128 devices in a mesh: group: 4 (over z), dev: 32 (over x, y, core).
Axes of the slice: x: 4, y: 4, z: 4, core: 2. Of those that a mesh axis runs over, the one named last changes fastest.
Arguments:
- embeddings: bfloat16 [128, 128, 1280], P(('group', 'dev')), may hold values from -8 to 8
- weight_q: bfloat16 [1280, 1280], replicated, may hold values from -0.15625 to 0.15625
- weight_k: bfloat16 [1280, 1280], replicated, may hold values from -0.15625 to 0.15625
- weight_v: bfloat16 [1280, 1280], replicated, may hold values from -0.15625 to 0.15625
- weight_o: bfloat16 [1280, 1280], replicated, may hold values from -0.15625 to 0.15625
- pairs: int32 [256, 2], replicated, may hold values from 0 to 127, as said below
- lengths: int32 [128], replicated, may hold values from 1 to 128, as said below
- holder: int32 [128], replicated, may hold values from 0 to 127, each once
Outputs:
- updated: bfloat16 [128, 128, 1280], P(('group', 'dev'))
The draws below stay inside these ranges and needn't reach their ends.
Inputs may be any that keep to these rules, and one draw needn't show every extreme that they name: `pairs`: the two proteins of a pair differ. `lengths`: some protein has exactly 128 residues.
All inputs are finite; a program needn't handle non-finite values.
Results may differ from the reference program's by a relative error of at most 0.02.
Values may be sent and summed in bfloat16 or wider, within the bound.
No kernel may reach another device: no remote copies, remote signals or barrier semaphores. Data moves between devices by JAX's collectives and lax.ppermute only.
A program may use at most 128 MiB of HBM per device.

```python
import jax
import jax.numpy as jnp
from jax import lax

D = 1280
HEADS = 20
HEAD_DIM = 64
LMAX = 128
PAIR_DEV = 2
NPROT = 128
PAIRS = 256
N_GROUP = 4
N_DEV = 32


def draw_pairs(key, part):
    key = jax.random.fold_in(key, 11)
    first_key, second_key = jax.random.split(key)
    first = jax.random.randint(first_key, (PAIRS,), 0, NPROT)
    offset = jax.random.randint(second_key, (PAIRS,), 1, NPROT)
    second = (first + offset) % NPROT
    return jnp.stack([first, second], axis=1).astype(jnp.int32)


def draw_lengths(key, part):
    key = jax.random.fold_in(key, 23)
    base_key, pick_key = jax.random.split(key)
    base = jax.random.randint(base_key, (NPROT,), 1, LMAX + 1)
    longest = jax.random.randint(pick_key, (), 0, NPROT)
    return jnp.where(jnp.arange(NPROT) == longest, LMAX, base).astype(jnp.int32)


def draw_embeddings(key, part):
    key = jax.random.fold_in(key, 37)
    base_key = jax.random.fold_in(key, 3)
    values = jax.random.truncated_normal(base_key, -6.0, 6.0, (NPROT, LMAX, D), jnp.float32)
    return values.astype(jnp.bfloat16)


def bell_draw(key, dims, width, limit, kind=jnp.bfloat16):
    return jnp.clip(width * jax.random.normal(key, dims, jnp.float32), -limit, limit).astype(kind)


def setup_inputs(seed: int = 0) -> dict:
    splits = jax.random.split(jax.random.key(seed), 9)
    return {
        "embeddings": draw_embeddings(jax.random.fold_in(splits[8], 71), 0),
        "weight_q": bell_draw(splits[1], (D, D), D ** -0.5, 0.15625),
        "weight_k": bell_draw(splits[2], (D, D), D ** -0.5, 0.15625),
        "weight_v": bell_draw(splits[3], (D, D), D ** -0.5, 0.15625),
        "weight_o": bell_draw(splits[4], (D, D), D ** -0.5, 0.15625),
        "pairs": draw_pairs(jax.random.fold_in(splits[8], 71), 0),
        "lengths": draw_lengths(jax.random.fold_in(splits[8], 71), 0),
        "holder": jax.random.permutation(splits[7], NPROT).astype(jnp.int32),
    }


def project(features_in, weight):
    flattened = features_in.reshape(-1, features_in.shape[-1])
    result = jnp.dot(flattened, weight, preferred_element_type=jnp.float32)
    return result.astype(jnp.bfloat16).reshape(features_in.shape)


def side_updates(query_rows, key_rows, value_rows, own_len, other_len, weight_o):
    sides, length, model_width = query_rows.shape
    heads_q = query_rows.reshape(sides, length, HEADS, HEAD_DIM).astype(jnp.float32)
    heads_k = key_rows.reshape(sides, length, HEADS, HEAD_DIM).astype(jnp.float32)
    heads_v = value_rows.reshape(sides, length, HEADS, HEAD_DIM).astype(jnp.float32)
    scores = jnp.einsum("nihd,njhd->nhij", heads_q, heads_k) * (HEAD_DIM ** -0.5)
    positions = jnp.arange(length, dtype=jnp.int32)
    key_live = positions[None, :] < other_len[:, None]
    scores = jnp.where(key_live[:, None, None, :], scores, -1e30)
    row_max = jnp.max(scores, axis=-1, keepdims=True)
    exponent = jnp.exp(scores - row_max)
    attention = (exponent / jnp.sum(exponent, axis=-1, keepdims=True)).astype(jnp.bfloat16)
    context = jnp.einsum("nhij,njhd->nihd", attention.astype(jnp.float32), heads_v).astype(jnp.bfloat16)
    updates = jnp.dot(context.reshape(sides * length, model_width), weight_o, preferred_element_type=jnp.float32)
    updates = updates.reshape(sides, length, model_width)
    query_live = positions[None, :] < own_len[:, None]
    return jnp.where(query_live[:, :, None], updates, 0.0)


def reference(embeddings, weight_q, weight_k, weight_v, weight_o, pairs, lengths, holder):
    query_all = project(embeddings, weight_q)
    key_all = project(embeddings, weight_k)
    value_all = project(embeddings, weight_v)

    def one_column(column, running):
        column = jnp.asarray(column).astype(jnp.int32)
        owners = jnp.arange(N_GROUP, dtype=jnp.int32) * N_DEV + column
        pair_rows = (owners[:, None] * PAIR_DEV + jnp.arange(PAIR_DEV, dtype=jnp.int32)[None, :]).reshape(-1)
        chosen = pairs[pair_rows]
        own_ids = chosen.reshape(-1)
        other_ids = chosen[:, ::-1].reshape(-1)
        own_rows = holder[own_ids]
        other_rows = holder[other_ids]
        updates = side_updates(query_all[own_rows], key_all[other_rows], value_all[other_rows],
                               lengths[own_ids], lengths[other_ids], weight_o)
        partial_value = jnp.zeros((NPROT, LMAX, D), jnp.float32).at[own_rows].add(updates)
        rounded = lax.optimization_barrier(partial_value.astype(jnp.bfloat16))
        return running + rounded.astype(jnp.float32)

    running = lax.fori_loop(0, N_DEV, one_column, jnp.zeros((NPROT, LMAX, D), jnp.float32))
    return (embeddings.astype(jnp.float32) + running).astype(jnp.bfloat16)
```

```python
import jax
import jax.numpy as jnp
from jax import lax
from jax.sharding import PartitionSpec as P

HEADS = 20
HEAD_DIM = 64
SLOTS = 4
AXES = ("group", "dev")


def exchange(array):
    return lax.all_to_all(array, AXES, split_axis=0, concat_axis=0, tiled=True)


def attend(query, key, value, other_len):
    rows, width = query.shape
    query = query.reshape(rows, HEADS, HEAD_DIM)
    key = key.reshape(rows, HEADS, HEAD_DIM)
    value = value.reshape(rows, HEADS, HEAD_DIM)
    scores = jnp.einsum("ihd,jhd->hij", query, key, preferred_element_type=jnp.float32)
    scores = scores * HEAD_DIM ** (-0.5)
    live = jnp.arange(rows, dtype=jnp.int32) < other_len
    scores = jnp.where(live[None, None, :], scores, -1e30)
    exponent = jnp.exp(scores - jnp.max(scores, axis=-1, keepdims=True))
    weights = (exponent / jnp.sum(exponent, axis=-1, keepdims=True)).astype(jnp.bfloat16)
    context = jnp.einsum("hij,jhd->ihd", weights, value, preferred_element_type=jnp.float32)
    return context.astype(jnp.bfloat16).reshape(rows, width)


def local(embeddings, weight_q, weight_k, weight_v, weight_o, pairs, lengths, holder):
    residues, width = embeddings.shape[1:]
    count = lax.axis_size("group") * lax.axis_size("dev")
    me = lax.axis_index("group") * lax.axis_size("dev") + lax.axis_index("dev")
    places = holder[pairs.reshape(-1)]
    selector = (places[:, None] == jnp.arange(count, dtype=jnp.int32)[None, :]).astype(jnp.bfloat16)
    mine = exchange(embeddings.reshape(residues, 1, width)).reshape(count, width)
    picked = jnp.dot(selector, mine, preferred_element_type=jnp.float32).astype(jnp.bfloat16)
    arrived = exchange(picked.reshape(count, SLOTS, width))
    features = jnp.swapaxes(arrived, 0, 1).reshape(SLOTS * residues, width)

    def project(weight):
        result = jnp.dot(features, weight, preferred_element_type=jnp.float32)
        return result.astype(jnp.bfloat16).reshape(SLOTS, residues, width)

    query, key, value = project(weight_q), project(weight_k), project(weight_v)
    ids = lax.dynamic_slice_in_dim(pairs.reshape(-1), me * SLOTS, SLOTS)
    lens = lengths[ids]
    contexts = [attend(query[s], key[s ^ 1], value[s ^ 1], lens[s ^ 1]) for s in range(SLOTS)]
    returned = exchange(jnp.stack(contexts, axis=1)).reshape(count * SLOTS, width)
    summed = lax.dot_general(
        selector, returned, (((0,), (0,)), ((), ())), preferred_element_type=jnp.float32
    ).astype(jnp.bfloat16)
    total = exchange(summed.reshape(count, 1, width)).reshape(residues, width)
    update = jnp.dot(total, weight_o, preferred_element_type=jnp.float32)
    own_len = jnp.sum(jnp.where(holder == me, lengths, 0))
    update = jnp.where(jnp.arange(residues, dtype=jnp.int32)[:, None] < own_len, update, 0.0)
    return (embeddings.astype(jnp.float32) + update[None]).astype(jnp.bfloat16)


def solution(mesh):
    in_specs = (P(AXES, None, None), P(), P(), P(), P(), P(), P(), P())
    out_specs = P(AXES, None, None)
    return jax.shard_map(local, mesh=mesh, in_specs=in_specs, out_specs=out_specs, check_vma=False)
```

```python
import functools

import jax
import jax.numpy as jnp
from jax import lax
from jax.experimental import pallas as pl
from jax.experimental.pallas import tpu as pltpu
from jax.sharding import PartitionSpec as P

HEAD_DIM = 64
AXES = ("group", "dev")
BLOCK = 64
UNITS = 16
BF = jnp.bfloat16
F32 = jnp.float32


def exchange(array):
    return lax.all_to_all(array, AXES, split_axis=0, concat_axis=0, tiled=True)


def swap(array):
    count = lax.axis_size("dev")
    return lax.ppermute(array, "dev", [(i, i ^ 1) for i in range(count)])


def mm(a, b):
    return jnp.dot(a, b, preferred_element_type=F32)


def plan(pairs, lengths, holder):
    own, other = pairs.reshape(-1), pairs[:, ::-1].reshape(-1)
    place, source, length = holder[own], holder[other], lengths[other]
    amount = 1 + (length > BLOCK).astype(jnp.int32)
    order = jnp.arange(own.shape[0], dtype=jnp.int32)
    earlier = order[:, None] < order[None, :]
    chip = place // 2
    same = chip[:, None] == chip[None, :]
    column = amount[:, None]
    before = jnp.sum(jnp.where(same & earlier, column, 0), axis=0)
    whole = jnp.sum(jnp.where(same, column, 0), axis=0)
    dest = 2 * chip + (2 * before + amount > whole).astype(jnp.int32)
    alike = (dest[:, None] == dest[None, :]) & earlier
    base = jnp.sum(jnp.where(alike, column, 0), axis=0)
    rank = jnp.sum(alike.astype(jnp.int32), axis=0)
    fits = jnp.max(base + amount) <= UNITS
    half = UNITS // 2
    turn = jnp.where(fits, 0, rank // half)
    slot = jnp.where(fits, rank, rank % half)
    base = jnp.where(fits, base, 2 * slot)
    return dest, source, length, amount, base, slot, turn, place % 2, jnp.max(turn) + 1


def attend_kernel(meta, got, query, weight_k, weight_v, out, rows, keys, values):
    width = weight_k.shape[0]
    half = width // 2
    lead = lax.broadcasted_iota(jnp.int32, (256, 256), 0)
    lane = lax.broadcasted_iota(jnp.int32, (256, 256), 1)
    turned = ((lead // 16 == lane % 16) & (lead % 16 == lane // 16)).astype(BF)
    for side in range(2):
        for part in range(BLOCK // 16):
            at = side * BLOCK + part * 16
            piece = mm(turned, got[at : at + 16].reshape(256, half)).astype(BF)
            for u in range(UNITS):
                to = u * BLOCK + part * 16
                rows[to : to + 16, side * half : (side + 1) * half] = piece[u * 16 : (u + 1) * 16]

    def project(chunk, carry):
        at = pl.ds(pl.multiple_of(chunk * 256, 256), 256)
        block = rows[at, :]
        keys[at, :] = mm(block, weight_k[...]).astype(BF)
        values[at, :] = mm(block, weight_v[...]).astype(BF)
        return carry

    lax.fori_loop(0, UNITS * BLOCK // 256, project, 0)
    tail = pl.ds(UNITS * BLOCK, BLOCK)
    keys[tail, :] = jnp.zeros((BLOCK, width), BF)
    values[tail, :] = jnp.zeros((BLOCK, width), BF)
    out[...] = jnp.zeros_like(out)
    first = lax.broadcasted_iota(jnp.int32, (128, 128), 1) < HEAD_DIM
    ones = jnp.ones((128, 128), BF)
    none = jnp.zeros((128, 128), BF)
    sums = jnp.concatenate([jnp.where(first, ones, none), jnp.where(first, none, ones)], axis=0)
    position = lax.broadcasted_iota(jnp.int32, (128, 128), 1)

    def item(index, carry):
        start = pl.multiple_of(meta[1 + index] * BLOCK, BLOCK)
        length = meta[1 + UNITS + index]
        whose = pl.multiple_of(meta[1 + 2 * UNITS + index] * 128, 128)
        live = position < length
        for pair in range(width // 128):
            at = slice(pair * 128, (pair + 1) * 128)
            q = query[pl.ds(whose, 128), at]
            k = keys[pl.ds(start, 128), at]
            v = values[pl.ds(start, 128), at]
            k2 = jnp.concatenate([jnp.where(first, k, none), jnp.where(first, none, k)], axis=0)
            v2 = jnp.concatenate([jnp.where(first, v, none), jnp.where(first, none, v)], axis=0)
            scores = lax.dot_general(q, k2, (((1,), (1,)), ((), ())), preferred_element_type=F32)
            parts = []
            for head in range(2):
                s = jnp.where(live, scores[:, head * 128 : (head + 1) * 128], -1e30)
                parts.append(jnp.exp(s - jnp.max(s, axis=1, keepdims=True)).astype(BF))
            weights = jnp.concatenate(parts, axis=1)
            result = mm(weights, jnp.concatenate([v2, sums], axis=1))
            out[pl.ds(whose, 128), at] += result[:, :128] / result[:, 128:]
        return carry

    lax.fori_loop(0, meta[0], item, 0)


def attend(meta, got, query, weight_k, weight_v):
    width = weight_k.shape[0]
    vmem = pl.BlockSpec(memory_space=pltpu.VMEM)
    return pl.pallas_call(
        attend_kernel,
        out_shape=jax.ShapeDtypeStruct((256, width), F32),
        in_specs=[pl.BlockSpec(memory_space=pltpu.SMEM)] + [vmem] * 4,
        out_specs=vmem,
        scratch_shapes=[
            pltpu.VMEM((UNITS * BLOCK, width), BF),
            pltpu.VMEM(((UNITS + 1) * BLOCK, width), BF),
            pltpu.VMEM(((UNITS + 1) * BLOCK, width), BF),
        ],
        compiler_params=pltpu.CompilerParams(vmem_limit_bytes=40 * 1024 * 1024),
        cost_estimate=pl.CostEstimate(flops=10**10, bytes_accessed=10**7, transcendentals=10**6),
    )(meta, got, query, weight_k, weight_v)


def local(embeddings, weight_q, weight_k, weight_v, weight_o, pairs, lengths, holder):
    residues, width = embeddings.shape[1:]
    half = width // 2
    count = lax.axis_size("group") * lax.axis_size("dev")
    me = lax.axis_index("group") * lax.axis_size("dev") + lax.axis_index("dev")
    own = embeddings[0]
    pieces = own.reshape(2, BLOCK, 2, half).transpose(2, 1, 0, 3).reshape(count, 2, half)
    mine = exchange(pieces).reshape(2 * count, half)
    query = mm(jnp.concatenate([own, swap(own)], axis=0), weight_q).astype(BF) * BF(HEAD_DIM**-0.5)
    dest, source, length, amount, base, slot, turn, core, rounds = plan(pairs, lengths, holder)
    spots = jnp.arange(UNITS, dtype=jnp.int32)
    devices = jnp.arange(count, dtype=jnp.int32)

    def one_round(number):
        active = turn == number
        target = ((dest[None, :] == devices[:, None]) & active[None, :]).astype(BF)
        entry = jnp.where(base[:, None] == spots[None, :], 2 * source[:, None] + 1, 0)
        second = (base[:, None] + 1 == spots[None, :]) & (amount[:, None] == 2)
        entry = jnp.where(second, 2 * source[:, None] + 2, entry)
        table = mm(target, entry.astype(BF)).astype(jnp.int32)
        units = 1 + jnp.arange(2 * count, dtype=jnp.int32)
        selector = (table.reshape(-1)[:, None] == units[None, :]).astype(BF)
        picked = mm(selector, mine).astype(BF)
        got = exchange(picked.reshape(count, UNITS, half))
        held = active & (dest == me)
        chosen = held[None, :] & (slot[None, :] == spots[:, None])

        def listed(values):
            return jnp.sum(jnp.where(chosen, values[None, :], 0), axis=1)

        number_held = jnp.sum(held.astype(jnp.int32)).reshape(1)
        whose = listed(core ^ (me % 2))
        meta = jnp.concatenate([number_held, listed(base), listed(length), whose])
        return attend(meta, got, query, weight_k, weight_v)

    total = one_round(0)
    _, total = lax.while_loop(
        lambda c: c[0] < rounds, lambda c: (c[0] + 1, c[1] + one_round(c[0])), (jnp.int32(1), total)
    )
    context = total[:residues] + swap(total[residues:].astype(BF)).astype(F32)
    update = mm(context.astype(BF), weight_o)
    own_len = jnp.sum(jnp.where(holder == me, lengths, 0))
    update = jnp.where(jnp.arange(residues, dtype=jnp.int32)[:, None] < own_len, update, 0.0)
    return (embeddings.astype(F32) + update[None]).astype(BF)


def solution(mesh):
    in_specs = (P(AXES, None, None), P(), P(), P(), P(), P(), P(), P())
    out_specs = P(AXES, None, None)
    return jax.shard_map(local, mesh=mesh, in_specs=in_specs, out_specs=out_specs, check_vma=False)
```

```python
import jax
import jax.numpy as jnp
from jax import lax
from jax.experimental import pallas as pl
from jax.experimental.pallas import tpu as pltpu
from jax.sharding import PartitionSpec as P

HEAD_DIM = 64
AXES = ("group", "dev")
BLOCK = 64
UNITS = 16
BF = jnp.bfloat16
F32 = jnp.float32


def exchange(array):
    return lax.all_to_all(array, AXES, split_axis=0, concat_axis=0, tiled=True)


def swap(array):
    count = lax.axis_size("dev")
    return lax.ppermute(array, "dev", [(i, i ^ 1) for i in range(count)])


def mm(a, b):
    return jnp.dot(a, b, preferred_element_type=F32)


def plan_kernel(place, pairs, lengths, holder, selector, meta, sides):
    me = place[0]
    count = pairs.shape[0]
    total = 2 * count
    devices = holder.shape[1]
    lane = lax.broadcasted_iota(jnp.int32, (count, devices), 1)
    marks = [pairs[:, i : i + 1] == lane for i in range(2)]
    held_at = holder[...].astype(F32)
    long = lengths[...].astype(F32)
    places = [jnp.sum(jnp.where(m, held_at, 0.0), axis=1, keepdims=True) for m in marks]
    sizes = [jnp.sum(jnp.where(m, long, 0.0), axis=1, keepdims=True) for m in marks]
    place_col = jnp.concatenate(places, axis=0)
    source_col = jnp.concatenate(places[::-1], axis=0)
    length_col = jnp.concatenate(sizes[::-1], axis=0)
    lane = lax.broadcasted_iota(jnp.int32, (total, devices), 1)
    listed = jnp.where(lane == 0, place_col, jnp.where(lane == 1, source_col, length_col))
    turned = jnp.transpose(listed).astype(jnp.int32)
    place_row, source, length = turned[0:1], turned[1:2], turned[2:3]
    amount = 1 + (length > BLOCK).astype(jnp.int32)
    amount_col = 1.0 + (length_col > BLOCK).astype(F32)
    chip = place_row // 2
    lead = lax.broadcasted_iota(jnp.int32, (total, total), 0)
    follow = lax.broadcasted_iota(jnp.int32, (total, total), 1)
    earlier = lead < follow
    same = place_col.astype(jnp.int32) // 2 == chip
    before = jnp.sum(jnp.where(same & earlier, amount_col, 0.0), axis=0, keepdims=True)
    whole = jnp.sum(jnp.where(same, amount_col, 0.0), axis=0, keepdims=True)
    later = 2.0 * before + amount.astype(F32) > whole
    dest = 2 * chip + later.astype(jnp.int32)
    dest_col = jnp.transpose(jnp.broadcast_to(dest.astype(F32), (devices, total)))[:, 0:1]
    alike = (dest_col.astype(jnp.int32) == dest) & earlier
    base = jnp.sum(jnp.where(alike, amount_col, 0.0), axis=0, keepdims=True).astype(jnp.int32)
    rank = jnp.sum(jnp.where(alike, 1.0, 0.0), axis=0, keepdims=True).astype(jnp.int32)
    half = UNITS // 2
    fits = jnp.max(base + amount, axis=1, keepdims=True) <= UNITS
    turn = jnp.where(fits, 0, rank // half)
    slot = jnp.where(fits, rank, rank % half)
    base = jnp.where(fits, base, 2 * slot)
    sides[...] = jnp.concatenate([dest, source, length, amount, base, slot, turn, place_row], axis=0)
    active = turn == 0
    spot = lax.broadcasted_iota(jnp.int32, (devices, total), 0)
    target = jnp.where((dest == spot) & active, 1.0, 0.0).astype(BF)
    entry = jnp.where(base == spot, 2 * source + 1, 0)
    entry = jnp.where((base + 1 == spot) & (amount == 2), 2 * source + 2, entry)
    across = (((1,), (1,)), ((), ()))
    table = lax.dot_general(target, entry.astype(F32).astype(BF), across, preferred_element_type=F32)
    row = lax.broadcasted_iota(jnp.int32, (devices * UNITS, devices), 0)
    lane = lax.broadcasted_iota(jnp.int32, (devices * UNITS, devices), 1)
    spread = mm(jnp.where(row // UNITS == lane, 1.0, 0.0).astype(BF), table.astype(BF))
    unit = jnp.sum(jnp.where(row % UNITS == lane, spread, 0.0), axis=1, keepdims=True)
    units = lax.broadcasted_iota(jnp.int32, selector.shape, 1)
    selector[...] = jnp.where(unit.astype(jnp.int32) == units + 1, 1.0, 0.0).astype(BF)
    held = active & (dest == me)
    spot = lax.broadcasted_iota(jnp.int32, (UNITS, total), 0)
    chosen = held & (slot == spot)

    def column(values):
        return jnp.sum(jnp.where(chosen, values.astype(F32), 0.0), axis=1, keepdims=True)

    whose = (place_row + me) % 2
    amount_held = jnp.sum(jnp.where(held, 1.0, 0.0), axis=1, keepdims=True)
    lane = lax.broadcasted_iota(jnp.int32, meta.shape, 1)
    listed = jnp.where(lane == 1, column(length), column(base))
    listed = jnp.where(lane == 2, column(whose), listed)
    meta[...] = jnp.where(lane == 3, amount_held, listed).astype(jnp.int32)


def plan(me, pairs, lengths, holder):
    devices = holder.shape[0]
    vmem = pl.BlockSpec(memory_space=pltpu.VMEM)
    return pl.pallas_call(
        plan_kernel,
        out_shape=(
            jax.ShapeDtypeStruct((devices * UNITS, 2 * devices), BF),
            jax.ShapeDtypeStruct((UNITS, 128), jnp.int32),
            jax.ShapeDtypeStruct((8, 2 * pairs.shape[0]), jnp.int32),
        ),
        in_specs=[pl.BlockSpec(memory_space=pltpu.SMEM)] + [vmem] * 3,
        out_specs=(vmem,) * 3,
        compiler_params=pltpu.CompilerParams(vmem_limit_bytes=24 * 1024 * 1024),
        cost_estimate=pl.CostEstimate(flops=10**9, bytes_accessed=10**6, transcendentals=0),
    )(me.reshape(1), pairs, lengths.reshape(1, -1), holder.reshape(1, -1))


def front_kernel(own, pieces):
    half = own.shape[1] // 2
    for side in range(2):
        for j in range(2):
            pieces[side * BLOCK : (side + 1) * BLOCK, j, :] = own[
                j * BLOCK : (j + 1) * BLOCK, side * half : (side + 1) * half
            ]


def front(own):
    rows, width = own.shape
    vmem = pl.BlockSpec(memory_space=pltpu.VMEM)
    return pl.pallas_call(
        front_kernel,
        out_shape=jax.ShapeDtypeStruct((rows, 2, width // 2), BF),
        in_specs=[vmem],
        out_specs=vmem,
    )(own)


def pick_kernel(selector, mine, picked):
    rows, _, half = mine.shape
    units = mine[...].reshape(2 * rows, half)

    def some(chunk, carry):
        at = pl.ds(pl.multiple_of(chunk * 512, 512), 512)
        picked[at, :] = mm(selector[at, :], units).astype(BF)
        return carry

    lax.fori_loop(0, selector.shape[0] // 512, some, 0)


def pick(selector, mine):
    vmem = pl.BlockSpec(memory_space=pltpu.VMEM)
    return pl.pallas_call(
        pick_kernel,
        out_shape=jax.ShapeDtypeStruct((selector.shape[0], mine.shape[2]), BF),
        in_specs=[vmem] * 2,
        out_specs=vmem,
        compiler_params=pltpu.CompilerParams(vmem_limit_bytes=24 * 1024 * 1024),
        cost_estimate=pl.CostEstimate(flops=10**9, bytes_accessed=10**7, transcendentals=0),
    )(selector, mine)


def attend_kernel(
    meta, got, query, weight_k, weight_v, weight_o, out, sibling, rows, keys, values, context
):
    width = weight_k.shape[0]
    half = width // 2
    lead = lax.broadcasted_iota(jnp.int32, (256, 256), 0)
    lane = lax.broadcasted_iota(jnp.int32, (256, 256), 1)
    turned = ((lead // 16 == lane % 16) & (lead % 16 == lane // 16)).astype(BF)
    for side in range(2):
        for part in range(BLOCK // 16):
            at = side * BLOCK + part * 16
            piece = mm(turned, got[at : at + 16].reshape(256, half)).astype(BF)
            for u in range(UNITS):
                to = u * BLOCK + part * 16
                rows[to : to + 16, side * half : (side + 1) * half] = piece[u * 16 : (u + 1) * 16]

    def project(chunk, carry):
        at = pl.ds(pl.multiple_of(chunk * 256, 256), 256)
        block = rows[at, :]
        keys[at, :] = mm(block, weight_k[...]).astype(BF)
        values[at, :] = mm(block, weight_v[...]).astype(BF)
        return carry

    lax.fori_loop(0, UNITS * BLOCK // 256, project, 0)
    tail = pl.ds(UNITS * BLOCK, BLOCK)
    keys[tail, :] = jnp.zeros((BLOCK, width), BF)
    values[tail, :] = jnp.zeros((BLOCK, width), BF)
    context[...] = jnp.zeros_like(context)
    first = lax.broadcasted_iota(jnp.int32, (128, 128), 1) < HEAD_DIM
    ones = jnp.ones((128, 128), BF)
    none = jnp.zeros((128, 128), BF)
    sums = jnp.concatenate([jnp.where(first, ones, none), jnp.where(first, none, ones)], axis=0)
    position = lax.broadcasted_iota(jnp.int32, (128, 128), 1)

    def item(index, carry):
        start = pl.multiple_of(meta[index, 0] * BLOCK, BLOCK)
        length = meta[index, 1]
        whose = pl.multiple_of(meta[index, 2] * 128, 128)
        live = position < length
        for pair in range(width // 128):
            at = slice(pair * 128, (pair + 1) * 128)
            q = query[pl.ds(whose, 128), at]
            k = keys[pl.ds(start, 128), at]
            v = values[pl.ds(start, 128), at]
            k2 = jnp.concatenate([jnp.where(first, k, none), jnp.where(first, none, k)], axis=0)
            v2 = jnp.concatenate([jnp.where(first, v, none), jnp.where(first, none, v)], axis=0)
            scores = lax.dot_general(q, k2, (((1,), (1,)), ((), ())), preferred_element_type=F32)
            parts = []
            for head in range(2):
                s = jnp.where(live, scores[:, head * 128 : (head + 1) * 128], -1e30)
                parts.append(jnp.exp(s - jnp.max(s, axis=1, keepdims=True)).astype(BF))
            weights = jnp.concatenate(parts, axis=1)
            result = mm(weights, jnp.concatenate([v2, sums], axis=1))
            context[pl.ds(whose, 128), at] += result[:, :128] / result[:, 128:]
        return carry

    lax.fori_loop(0, meta[0, 3], item, 0)
    update = mm(context[...].astype(BF), weight_o[...])
    out[...] = update[:128]
    sibling[...] = update[128:].astype(BF)


def attend(meta, got, query, weight_k, weight_v, weight_o):
    width = weight_k.shape[0]
    vmem = pl.BlockSpec(memory_space=pltpu.VMEM)
    return pl.pallas_call(
        attend_kernel,
        out_shape=(
            jax.ShapeDtypeStruct((128, width), F32),
            jax.ShapeDtypeStruct((128, width), BF),
        ),
        in_specs=[pl.BlockSpec(memory_space=pltpu.SMEM)] + [vmem] * 5,
        out_specs=(vmem, vmem),
        scratch_shapes=[
            pltpu.VMEM((UNITS * BLOCK, width), BF),
            pltpu.VMEM(((UNITS + 1) * BLOCK, width), BF),
            pltpu.VMEM(((UNITS + 1) * BLOCK, width), BF),
            pltpu.VMEM((256, width), F32),
        ],
        compiler_params=pltpu.CompilerParams(vmem_limit_bytes=40 * 1024 * 1024),
        cost_estimate=pl.CostEstimate(flops=10**10, bytes_accessed=10**7, transcendentals=10**6),
    )(meta, got, query, weight_k, weight_v, weight_o)


def later_round(number, sides, me, count):
    dest, source, length, amount, base, slot, turn, place = sides
    spots = jnp.arange(UNITS, dtype=jnp.int32)
    active = turn == number
    target = (dest[None, :] == jnp.arange(count, dtype=jnp.int32)[:, None]) & active[None, :]
    entry = jnp.where(base[:, None] == spots[None, :], 2 * source[:, None] + 1, 0)
    second = (base[:, None] + 1 == spots[None, :]) & (amount[:, None] == 2)
    entry = jnp.where(second, 2 * source[:, None] + 2, entry)
    table = mm(target.astype(BF), entry.astype(BF)).astype(jnp.int32)
    units = 1 + jnp.arange(2 * count, dtype=jnp.int32)
    selector = (table.reshape(-1)[:, None] == units[None, :]).astype(BF)
    held = active & (dest == me)
    chosen = held[None, :] & (slot[None, :] == spots[:, None])

    def listed(values):
        return jnp.sum(jnp.where(chosen, values[None, :], 0), axis=1)

    amount_held = jnp.broadcast_to(jnp.sum(held.astype(jnp.int32)), (UNITS,))
    columns = [listed(base), listed(length), listed((place + me) % 2), amount_held]
    meta = jnp.stack(columns, axis=1)
    return selector, jnp.pad(meta, ((0, 0), (0, 124)))


def local(embeddings, weight_q, weight_k, weight_v, weight_o, pairs, lengths, holder):
    residues, width = embeddings.shape[1:]
    count = lax.axis_size("group") * lax.axis_size("dev")
    me = lax.axis_index("group") * lax.axis_size("dev") + lax.axis_index("dev")
    own = embeddings[0]
    mine = exchange(front(own))
    selector, meta, sides = plan(me, pairs, lengths, holder)
    rounds = jnp.max(sides[6]) + 1
    both = jnp.concatenate([own, swap(own)], axis=0)
    query = (mm(both, weight_q) * HEAD_DIM**-0.5).astype(BF)

    def one_round(selector, meta):
        got = exchange(pick(selector, mine).reshape(count, UNITS, width // 2))
        return attend(meta, got, query, weight_k, weight_v, weight_o)

    def another(carry):
        number, kept, given = carry
        more, also = one_round(*later_round(number, sides, me, count))
        given = (given.astype(F32) + also.astype(F32)).astype(BF)
        return number + 1, kept + more, given

    kept, given = one_round(selector, meta)
    _, kept, given = lax.while_loop(lambda c: c[0] < rounds, another, (jnp.int32(1), kept, given))
    update = kept + swap(given).astype(F32)
    own_len = jnp.sum(jnp.where(holder == me, lengths, 0))
    update = jnp.where(jnp.arange(residues, dtype=jnp.int32)[:, None] < own_len, update, 0.0)
    return (embeddings.astype(F32) + update[None]).astype(BF)


def solution(mesh):
    in_specs = (P(AXES, None, None), P(), P(), P(), P(), P(), P(), P())
    out_specs = P(AXES, None, None)
    return jax.shard_map(local, mesh=mesh, in_specs=in_specs, out_specs=out_specs, check_vma=False)
```

```python
import jax
import jax.numpy as jnp
from jax import lax
from jax.experimental import pallas as pl
from jax.experimental.pallas import tpu as pltpu
from jax.sharding import PartitionSpec as P

HEAD_DIM = 64
AXES = ("group", "dev")
BLOCK = 32
PARTS = 4
FIRST = 24
LATER = 16
STEP = LATER - PARTS + 1
MIB = 1024 * 1024
BF = jnp.bfloat16
F32 = jnp.float32
VMEM = pl.BlockSpec(memory_space=pltpu.VMEM)
SMEM = pl.BlockSpec(memory_space=pltpu.SMEM)
ANY = pl.BlockSpec(memory_space=pl.ANY)
ACROSS = (((1,), (1,)), ((), ()))
DOWN = (((0,), (0,)), ((), ()))


def exchange(array):
    return lax.all_to_all(array, AXES, split_axis=0, concat_axis=0, tiled=True)


def swap(array):
    count = lax.axis_size("dev")
    return lax.ppermute(array, "dev", [(i, i ^ 1) for i in range(count)])


def mm(a, b):
    return jnp.dot(a, b, preferred_element_type=F32)


def iota(shape, dim):
    return lax.broadcasted_iota(jnp.int32, shape, dim)


def half_turn(array):
    return pltpu.roll(array.astype(F32), 64, 1)


def front_kernel(own, pieces):
    low = iota((BLOCK, 128), 1) < 64
    for quarter in range(4):
        main = slice(256 * quarter, 256 * quarter + 256)
        tile = slice(1024 + 128 * (quarter // 2), 1152 + 128 * (quarter // 2))
        for h in range(2):
            even = slice(2 * h * BLOCK, (2 * h + 1) * BLOCK)
            odd = slice((2 * h + 1) * BLOCK, (2 * h + 2) * BLOCK)
            if quarter % 2 == 0:
                rest = jnp.where(low, own[even, tile].astype(F32), half_turn(own[odd, tile]))
            else:
                rest = jnp.where(low, half_turn(own[even, tile]), own[odd, tile].astype(F32))
            to = slice(quarter * BLOCK, (quarter + 1) * BLOCK)
            pieces[to, h, 0:256] = own[even, main]
            pieces[to, h, 256:512] = own[odd, main]
            pieces[to, h, 512:640] = rest.astype(BF)


def front(own):
    rows, width = own.shape
    return pl.pallas_call(
        front_kernel,
        out_shape=jax.ShapeDtypeStruct((rows, 2, width // 2), BF),
        in_specs=[VMEM],
        out_specs=VMEM,
        compiler_params=pltpu.CompilerParams(vmem_limit_bytes=4 * MIB),
    )(own)


def plan_kernel(place, pairs, lengths, holder, selector, meta, sides):
    me = place[0]
    count = pairs.shape[0]
    total = 2 * count
    devices = holder.shape[1]
    lane = iota((count, devices), 1)
    marks = [pairs[:, i : i + 1] == lane for i in range(2)]
    held_at = holder[...].astype(F32)
    long = lengths[...].astype(F32)
    places = [jnp.sum(jnp.where(m, held_at, 0.0), axis=1, keepdims=True) for m in marks]
    sizes = [jnp.sum(jnp.where(m, long, 0.0), axis=1, keepdims=True) for m in marks]
    place_col = jnp.concatenate(places, axis=0)
    source_col = jnp.concatenate(places[::-1], axis=0)
    length_col = jnp.concatenate(sizes[::-1], axis=0)
    lane = iota((total, devices), 1)
    listed = jnp.where(lane == 0, place_col, jnp.where(lane == 1, source_col, length_col))
    turned = jnp.transpose(listed).astype(jnp.int32)
    place_row, source, length = turned[0:1], turned[1:2], turned[2:3]
    amount = (length + (BLOCK - 1)) // BLOCK
    amount_col = ((length_col.astype(jnp.int32) + (BLOCK - 1)) // BLOCK).astype(F32)
    chip = place_row // 2
    earlier = iota((total, total), 0) < iota((total, total), 1)
    same = place_col.astype(jnp.int32) // 2 == chip
    before = jnp.sum(jnp.where(same & earlier, amount_col, 0.0), axis=0, keepdims=True)
    whole = jnp.sum(jnp.where(same, amount_col, 0.0), axis=0, keepdims=True)
    second = 2.0 * before + amount.astype(F32) > whole
    dest = 2 * chip + second.astype(jnp.int32)
    dest_col = jnp.transpose(jnp.broadcast_to(dest.astype(F32), (devices, total)))[:, 0:1]
    alike = (dest_col.astype(jnp.int32) == dest) & earlier
    base = jnp.sum(jnp.where(alike, amount_col, 0.0), axis=0, keepdims=True).astype(jnp.int32)
    slot = jnp.sum(jnp.where(alike, 1.0, 0.0), axis=0, keepdims=True).astype(jnp.int32)
    sides[...] = jnp.concatenate(
        [dest, source, length, amount, base, slot, place_row, place_row], axis=0
    )
    active = base + amount <= FIRST
    spot = iota((devices, total), 0)
    target = jnp.where((dest == spot) & active, 1.0, 0.0).astype(BF)
    there = (base <= spot) & (spot < base + amount)
    entry = jnp.where(there, source + 1, 0)
    shifted = spot - 64
    entry = entry + jnp.where((base <= shifted) & (shifted < base + amount), shifted - base, 0)
    table = lax.dot_general(target, entry.astype(F32).astype(BF), ACROSS, preferred_element_type=F32)
    rows = devices * FIRST // 2
    row, lane = iota((rows, devices), 0), iota((rows, devices), 1)
    which, v = lax.div(row, jnp.int32(FIRST // 2)), lax.rem(row, jnp.int32(FIRST // 2))
    spread = mm(jnp.where(which == lane, 1.0, 0.0).astype(BF), table.astype(BF))
    columns = iota((rows, 4 * devices), 1)
    unit_at = 2 * (columns % (2 * devices)) + columns // (2 * devices)
    for side in range(2):
        u = 2 * v + side
        value = jnp.where(lane == u, 4.0 * spread, jnp.where(lane == u + 64, spread, 0.0))
        unit = jnp.sum(value, axis=1, keepdims=True).astype(jnp.int32) - 4
        at = slice(side * 4 * devices, (side + 1) * 4 * devices)
        selector[:, at] = jnp.where(unit == unit_at, 1.0, 0.0).astype(BF)
    held = active & (dest == me)
    chosen = held & (slot == iota((FIRST, total), 0))

    def column(values):
        return jnp.sum(jnp.where(chosen, values.astype(F32), 0.0), axis=1, keepdims=True)

    amount_held = jnp.sum(jnp.where(held, 1.0, 0.0), axis=1, keepdims=True)
    rounds = jnp.max(jnp.where(active, 0, 1 + (base - (FIRST - PARTS + 1)) // STEP), axis=1, keepdims=True)
    ends = [
        jnp.sum(jnp.where(holder[...] == which, long, 0.0), axis=1, keepdims=True)
        for which in (me, me + 1 - 2 * (me % 2))
    ]
    lane = iota(meta.shape, 1)
    listed = jnp.where(lane == 1, column(length), column(base))
    listed = jnp.where(lane == 2, column((place_row + me) % 2), listed)
    listed = jnp.where(lane == 3, amount_held, listed)
    listed = jnp.where(lane == 4, ends[0], jnp.where(lane == 5, ends[1], listed))
    meta[...] = jnp.where(lane == 6, rounds.astype(F32), listed).astype(jnp.int32)


def plan(me, pairs, lengths, holder):
    devices = holder.shape[0]
    return pl.pallas_call(
        plan_kernel,
        out_shape=(
            jax.ShapeDtypeStruct((devices * FIRST // 2, 8 * devices), BF),
            jax.ShapeDtypeStruct((FIRST, 128), jnp.int32),
            jax.ShapeDtypeStruct((8, 2 * pairs.shape[0]), jnp.int32),
        ),
        in_specs=[SMEM] + [VMEM] * 3,
        out_specs=(VMEM,) * 3,
        compiler_params=pltpu.CompilerParams(vmem_limit_bytes=16 * MIB),
        cost_estimate=pl.CostEstimate(flops=10**9, bytes_accessed=10**6, transcendentals=0),
    )(me.reshape(1), pairs, lengths.reshape(1, -1), holder.reshape(1, -1))


def pick_kernel(selector, mine, picked):
    rows, _, half = mine.shape
    units = mine[...].reshape(2 * rows, half)
    ends = units[:, 512:640].astype(F32)
    turned = half_turn(ends)
    low = iota(ends.shape, 1) < 64
    nil = jnp.zeros_like(ends)
    main = jnp.concatenate([units[:, 0:256], units[:, 256:512]], axis=0)
    ends_low = jnp.concatenate([jnp.where(low, ends, nil), jnp.where(low, turned, nil)], axis=0)
    ends_high = jnp.concatenate([jnp.where(low, nil, turned), jnp.where(low, nil, ends)], axis=0)
    even = jnp.concatenate([main, ends_low.astype(BF)], axis=1)
    odd = jnp.concatenate([main, ends_high.astype(BF)], axis=1)
    outer = picked.shape[1:-1]
    each = 1
    for n in outer:
        each *= n

    def some(chunk, carry):
        at = pl.ds(pl.multiple_of(chunk * (32 * each), 32 * each), 32 * each)
        first = mm(selector[at, : 4 * rows], even)
        second = mm(selector[at, 4 * rows :], odd)
        rest = first[:, 256:] + second[:, 256:]
        message = jnp.concatenate([first[:, :256], second[:, :256], rest], axis=1).astype(BF)
        picked[pl.ds(chunk * 32, 32)] = message.reshape((32,) + outer + (half,))
        return carry

    lax.fori_loop(0, rows // 32, some, 0)


def pick(selector, mine, outer):
    devices, _, half = mine.shape
    return pl.pallas_call(
        pick_kernel,
        out_shape=jax.ShapeDtypeStruct((devices,) + outer + (half,), BF),
        in_specs=[VMEM] * 2,
        out_specs=VMEM,
        compiler_params=pltpu.CompilerParams(vmem_limit_bytes=16 * MIB),
        cost_estimate=pl.CostEstimate(flops=10**9, bytes_accessed=10**7, transcendentals=0),
    )(selector, mine)


def query_kernel(own, other, weight, query):
    first = iota((128, 128), 1) < HEAD_DIM
    none = jnp.zeros((128, 128), BF)
    for who, rows in enumerate((own, other)):
        result = (mm(rows[...], weight[...]).astype(BF)) * BF(HEAD_DIM**-0.5)
        for pair in range(result.shape[1] // 128):
            at = (who * (result.shape[1] // 128) + pair) * 256
            tile = result[:, pair * 128 : (pair + 1) * 128]
            query[at : at + 128, :] = jnp.where(first, tile, none)
            query[at + 128 : at + 256, :] = jnp.where(first, none, tile)


def queries(own, other, weight):
    return pl.pallas_call(
        query_kernel,
        out_shape=jax.ShapeDtypeStruct((4 * own.shape[1], 128), BF),
        in_specs=[VMEM] * 3,
        out_specs=VMEM,
        compiler_params=pltpu.CompilerParams(vmem_limit_bytes=12 * MIB),
        cost_estimate=pl.CostEstimate(flops=10**9, bytes_accessed=10**7, transcendentals=0),
    )(own, other, weight)


def attend_kernel(
    meta, got_at, query_at, k_at, v_at, o_at, out, sibling,
    got, query, weight_k, weight_v, weight_o, rows, keys, values, context, sems,
):
    copies = [
        pltpu.make_async_copy(a, b, sems.at[i])
        for i, (a, b) in enumerate(
            [(got_at, got), (k_at, weight_k), (v_at, weight_v), (query_at, query), (o_at, weight_o)]
        )
    ]
    for copy in copies:
        copy.start()
    width = weight_k.shape[0]
    each = 1
    for n in got.shape[1:-1]:
        each *= n
    tall = 16 * each
    context[...] = jnp.zeros_like(context)
    tail = pl.ds(2 * each * BLOCK, (PARTS - 1) * BLOCK)
    keys[tail, :] = jnp.zeros(((PARTS - 1) * BLOCK, width), BF)
    values[tail, :] = jnp.zeros(((PARTS - 1) * BLOCK, width), BF)
    lead, lane = iota((tall, tall), 0), iota((tall, tall), 1)
    n = jnp.int32(each)
    turned = (lead == lax.rem(lane, n) * 16 + lax.div(lane, n)).astype(BF)
    low = iota((tall, 128), 1) < 64
    copies[0].wait()
    for part in range(2):
        rests = []
        for quarter in range(4):
            at = quarter * BLOCK + part * 16
            piece = mm(turned, got[at : at + 16].reshape(tall, width // 2))
            rests.append(piece[:, 512:640])
            piece = piece.astype(BF)
            for u in range(2 * each):
                to = u * BLOCK + part * 16
                side = (u % 2) * 256
                rows[to : to + 16, quarter * 256 : quarter * 256 + 256] = piece[
                    (u // 2) * 16 : (u // 2) * 16 + 16, side : side + 256
                ]
            if quarter % 2 == 1:
                left, right = rests[-2:]
                even = jnp.where(low, left, half_turn(right)).astype(BF)
                odd = jnp.where(low, half_turn(left), right).astype(BF)
                tile = 1024 + 128 * (quarter // 2)
                for u in range(2 * each):
                    to = u * BLOCK + part * 16
                    rows[to : to + 16, tile : tile + 128] = (odd if u % 2 else even)[
                        (u // 2) * 16 : (u // 2) * 16 + 16
                    ]
    copies[1].wait()
    copies[2].wait()

    def project(chunk, carry):
        at = pl.ds(pl.multiple_of(chunk * 256, 256), 256)
        block = rows[at, :]
        keys[at, :] = mm(block, weight_k[...]).astype(BF)
        values[at, :] = mm(block, weight_v[...]).astype(BF)
        return carry

    lax.fori_loop(0, 2 * each * BLOCK // 256, project, 0)
    copies[3].wait()

    def item(index, carry):
        start = pl.multiple_of(meta[index, 0] * BLOCK, BLOCK)
        length = meta[index, 1]
        whose = meta[index, 2]

        def with_keys(size):
            live = iota((size, 256), 0) < length
            span = pl.ds(start, size)
            for pair in range(width // 128):
                at = slice(pair * 128, (pair + 1) * 128)
                q = query[pl.ds(pl.multiple_of(whose * (2 * width) + pair * 256, 256), 256), :]
                scores = lax.dot_general(keys[span, at], q, ACROSS, preferred_element_type=F32)
                scores = jnp.where(live, scores, -1e30)
                weights = jnp.exp(scores - jnp.max(scores, axis=0, keepdims=True))
                scale = 1.0 / jnp.sum(weights, axis=0, keepdims=True)
                result = lax.dot_general(
                    values[span, at], weights.astype(BF), DOWN, preferred_element_type=F32
                )
                to = pl.multiple_of(whose * width + pair * 128, 128)
                context[pl.ds(to, 64), :] += result[:64, :128] * scale[:, :128]
                context[pl.ds(to + 64, 64), :] += result[64:, 128:] * scale[:, 128:]

        @pl.when(length <= 64)
        def _():
            with_keys(64)

        @pl.when(length > 64)
        def _():
            with_keys(128)

        return carry

    lax.fori_loop(0, meta[0, 3], item, 0)
    copies[4].wait()
    for who, to in enumerate((out, sibling)):
        part = context[who * width : (who + 1) * width, :].astype(BF)
        update = lax.dot_general(part, weight_o[...], DOWN, preferred_element_type=F32)
        update = jnp.where(iota(update.shape, 0) < meta[0, 4 + who], update, 0.0)
        to[...] = update.astype(to.dtype)


def attend(meta, got, query, weight_k, weight_v, weight_o):
    width = weight_k.shape[0]
    each = 1
    for n in got.shape[1:-1]:
        each *= n
    tall = 2 * each * BLOCK
    return pl.pallas_call(
        attend_kernel,
        out_shape=(
            jax.ShapeDtypeStruct((128, width), F32),
            jax.ShapeDtypeStruct((128, width), BF),
        ),
        in_specs=[SMEM] + [ANY] * 5,
        out_specs=(VMEM, VMEM),
        scratch_shapes=[
            pltpu.VMEM(got.shape, BF),
            pltpu.VMEM(query.shape, BF),
            pltpu.VMEM((width, width), BF),
            pltpu.VMEM((width, width), BF),
            pltpu.VMEM((width, width), BF),
            pltpu.VMEM((tall, width), BF),
            pltpu.VMEM((tall + (PARTS - 1) * BLOCK, width), BF),
            pltpu.VMEM((tall + (PARTS - 1) * BLOCK, width), BF),
            pltpu.VMEM((2 * width, 128), F32),
            pltpu.SemaphoreType.DMA((5,)),
        ],
        compiler_params=pltpu.CompilerParams(vmem_limit_bytes=36 * MIB),
        cost_estimate=pl.CostEstimate(flops=10**10, bytes_accessed=10**7, transcendentals=10**6),
    )(meta, got, query, weight_k, weight_v, weight_o)


def later_round(number, sides, me, count, meta):
    dest, source, length, amount, base, _, place, _ = sides
    origin = FIRST - PARTS + 1
    turn = jnp.where(base + amount <= FIRST, 0, 1 + (base - origin) // STEP)
    active = turn == number
    base = base - origin - (number - 1) * STEP
    spots = jnp.arange(LATER, dtype=jnp.int32)
    target = (dest[None, :] == jnp.arange(count, dtype=jnp.int32)[:, None]) & active[None, :]
    there = (base[:, None] <= spots) & (spots < (base + amount)[:, None])
    entries = [jnp.where(there, source[:, None] + 1, 0), jnp.where(there, spots - base[:, None], 0)]
    high, low = (mm(target.astype(BF), entry.astype(BF)).astype(jnp.int32) for entry in entries)
    unit = (4 * (high - 1) + low).reshape(-1, 2)
    columns = jnp.arange(4 * count, dtype=jnp.int32)
    unit_at = 2 * (columns % (2 * count)) + columns // (2 * count)
    selector = (unit[:, :, None] == unit_at).reshape(unit.shape[0], -1).astype(BF)
    held = active & (dest == me)
    order = jnp.cumsum(held.astype(jnp.int32)) - 1
    chosen = held[None, :] & (order[None, :] == spots[:, None])

    def listed(values):
        return jnp.sum(jnp.where(chosen, values[None, :], 0), axis=1)

    held_count = jnp.broadcast_to(jnp.sum(held.astype(jnp.int32)), (LATER,))
    columns = [listed(base), listed(length), listed((place + me) % 2), held_count]
    return selector, meta[:LATER].at[:, :4].set(jnp.stack(columns, axis=1))


def local(embeddings, weight_q, weight_k, weight_v, weight_o, pairs, lengths, holder):
    count = lax.axis_size("group") * lax.axis_size("dev")
    me = lax.axis_index("group") * lax.axis_size("dev") + lax.axis_index("dev")
    own = embeddings[0]
    mine = exchange(front(own))
    selector, meta, sides = plan(me, pairs, lengths, holder)
    query = queries(own, swap(own), weight_q)

    def one_round(selector, meta, outer):
        got = exchange(pick(selector, mine, outer))
        return attend(meta, got, query, weight_k, weight_v, weight_o)

    def another(carry):
        number, total = carry
        kept, given = one_round(*later_round(number, sides, me, count, meta), (LATER // 2,))
        return number + 1, total + kept + swap(given).astype(F32)

    kept, given = one_round(selector, meta, (FIRST // 8, 4))
    received = swap(given)
    _, kept = lax.while_loop(lambda c: c[0] <= meta[0, 6], another, (jnp.int32(1), kept))
    return (own.astype(F32) + (kept + received.astype(F32))).astype(BF)[None]


def solution(mesh):
    in_specs = (P(AXES, None, None), P(), P(), P(), P(), P(), P(), P())
    out_specs = P(AXES, None, None)
    return jax.shard_map(local, mesh=mesh, in_specs=in_specs, out_specs=out_specs, check_vma=False)
```

```python
import jax
import jax.numpy as jnp
from jax import lax
from jax.experimental import pallas as pl
from jax.experimental.pallas import tpu as pltpu
from jax.sharding import PartitionSpec as P

HEAD_DIM = 64
AXES = ("group", "dev")
BLOCK = 32
PARTS = 4
FIRST = 24
LATER = 16
STEP = LATER - PARTS + 1
MIB = 1024 * 1024
BF = jnp.bfloat16
F32 = jnp.float32
VMEM = pl.BlockSpec(memory_space=pltpu.VMEM)
SMEM = pl.BlockSpec(memory_space=pltpu.SMEM)
ANY = pl.BlockSpec(memory_space=pl.ANY)
ACROSS = (((1,), (1,)), ((), ()))
DOWN = (((0,), (0,)), ((), ()))


def exchange(array):
    return lax.all_to_all(array, AXES, split_axis=0, concat_axis=0, tiled=True)


def swap(array):
    count = lax.axis_size("dev")
    return lax.ppermute(array, "dev", [(i, i ^ 1) for i in range(count)])


def mm(a, b):
    return jnp.dot(a, b, preferred_element_type=F32)


def iota(shape, dim):
    return lax.broadcasted_iota(jnp.int32, shape, dim)


def half_turn(array):
    return pltpu.roll(array.astype(F32), 64, 1)


def front_kernel(own, pieces):
    low = iota((BLOCK, 128), 1) < 64
    for quarter in range(4):
        main = slice(256 * quarter, 256 * quarter + 256)
        tile = slice(1024 + 128 * (quarter // 2), 1152 + 128 * (quarter // 2))
        for h in range(2):
            even = slice(2 * h * BLOCK, (2 * h + 1) * BLOCK)
            odd = slice((2 * h + 1) * BLOCK, (2 * h + 2) * BLOCK)
            if quarter % 2 == 0:
                rest = jnp.where(low, own[even, tile].astype(F32), half_turn(own[odd, tile]))
            else:
                rest = jnp.where(low, half_turn(own[even, tile]), own[odd, tile].astype(F32))
            to = slice(quarter * BLOCK, (quarter + 1) * BLOCK)
            pieces[to, h, 0:256] = own[even, main]
            pieces[to, h, 256:512] = own[odd, main]
            pieces[to, h, 512:640] = rest.astype(BF)


def front(own):
    rows, width = own.shape
    return pl.pallas_call(
        front_kernel,
        out_shape=jax.ShapeDtypeStruct((rows, 2, width // 2), BF),
        in_specs=[VMEM],
        out_specs=VMEM,
        compiler_params=pltpu.CompilerParams(vmem_limit_bytes=4 * MIB),
    )(own)


def plan_kernel(place, pairs, lengths, holder, selector, meta, sides):
    me = place[0]
    count = pairs.shape[0]
    total = 2 * count
    devices = holder.shape[1]
    lane = iota((count, devices), 1)
    marks = [pairs[:, i : i + 1] == lane for i in range(2)]
    held_at = holder[...].astype(F32)
    long = lengths[...].astype(F32)
    places = [jnp.sum(jnp.where(m, held_at, 0.0), axis=1, keepdims=True) for m in marks]
    sizes = [jnp.sum(jnp.where(m, long, 0.0), axis=1, keepdims=True) for m in marks]
    place_col = jnp.concatenate(places, axis=0)
    source_col = jnp.concatenate(places[::-1], axis=0)
    length_col = jnp.concatenate(sizes[::-1], axis=0)
    lane = iota((total, devices), 1)
    listed = jnp.where(lane == 0, place_col, jnp.where(lane == 1, source_col, length_col))
    turned = jnp.transpose(listed).astype(jnp.int32)
    place_row, source, length = turned[0:1], turned[1:2], turned[2:3]
    amount = (length + (BLOCK - 1)) // BLOCK
    amount_col = ((length_col.astype(jnp.int32) + (BLOCK - 1)) // BLOCK).astype(F32)
    chip = place_row // 2
    earlier = iota((total, total), 0) < iota((total, total), 1)
    same = place_col.astype(jnp.int32) // 2 == chip
    before = jnp.sum(jnp.where(same & earlier, amount_col, 0.0), axis=0, keepdims=True)
    whole = jnp.sum(jnp.where(same, amount_col, 0.0), axis=0, keepdims=True)
    second = 2.0 * before + amount.astype(F32) > whole
    dest = 2 * chip + second.astype(jnp.int32)
    dest_col = jnp.transpose(jnp.broadcast_to(dest.astype(F32), (devices, total)))[:, 0:1]
    alike = (dest_col.astype(jnp.int32) == dest) & earlier
    base = jnp.sum(jnp.where(alike, amount_col, 0.0), axis=0, keepdims=True).astype(jnp.int32)
    slot = jnp.sum(jnp.where(alike, 1.0, 0.0), axis=0, keepdims=True).astype(jnp.int32)
    sides[...] = jnp.concatenate(
        [dest, source, length, amount, base, slot, place_row, place_row], axis=0
    )
    active = base + amount <= FIRST
    spot = iota((devices, total), 0)
    target = jnp.where((dest == spot) & active, 1.0, 0.0).astype(BF)
    there = (base <= spot) & (spot < base + amount)
    entry = jnp.where(there, source + 1, 0)
    shifted = spot - 64
    entry = entry + jnp.where((base <= shifted) & (shifted < base + amount), shifted - base, 0)
    table = lax.dot_general(target, entry.astype(F32).astype(BF), ACROSS, preferred_element_type=F32)
    rows = devices * FIRST // 2
    row, lane = iota((rows, devices), 0), iota((rows, devices), 1)
    which, v = lax.div(row, jnp.int32(FIRST // 2)), lax.rem(row, jnp.int32(FIRST // 2))
    spread = mm(jnp.where(which == lane, 1.0, 0.0).astype(BF), table.astype(BF))
    columns = iota((rows, 4 * devices), 1)
    unit_at = 2 * (columns % (2 * devices)) + columns // (2 * devices)
    for side in range(2):
        u = 2 * v + side
        value = jnp.where(lane == u, 4.0 * spread, jnp.where(lane == u + 64, spread, 0.0))
        unit = jnp.sum(value, axis=1, keepdims=True).astype(jnp.int32) - 4
        at = slice(side * 4 * devices, (side + 1) * 4 * devices)
        selector[:, at] = jnp.where(unit == unit_at, 1.0, 0.0).astype(BF)
    held = active & (dest == me)
    chosen = held & (slot == iota((FIRST, total), 0))

    def column(values):
        return jnp.sum(jnp.where(chosen, values.astype(F32), 0.0), axis=1, keepdims=True)

    amount_held = jnp.sum(jnp.where(held, 1.0, 0.0), axis=1, keepdims=True)
    rounds = jnp.max(jnp.where(active, 0, 1 + (base - (FIRST - PARTS + 1)) // STEP), axis=1, keepdims=True)
    ends = [
        jnp.sum(jnp.where(holder[...] == which, long, 0.0), axis=1, keepdims=True)
        for which in (me, me + 1 - 2 * (me % 2))
    ]
    lane = iota(meta.shape, 1)
    listed = jnp.where(lane == 1, column(length), column(base))
    listed = jnp.where(lane == 2, column((place_row + me) % 2), listed)
    listed = jnp.where(lane == 3, amount_held, listed)
    blocks = jnp.max(jnp.where(held, base + amount, 0), axis=1, keepdims=True).astype(F32)
    listed = jnp.where(lane == 7, blocks, listed)
    listed = jnp.where(lane == 4, ends[0], jnp.where(lane == 5, ends[1], listed))
    meta[...] = jnp.where(lane == 6, rounds.astype(F32), listed).astype(jnp.int32)


def plan(me, pairs, lengths, holder):
    devices = holder.shape[0]
    return pl.pallas_call(
        plan_kernel,
        out_shape=(
            jax.ShapeDtypeStruct((devices * FIRST // 2, 8 * devices), BF),
            jax.ShapeDtypeStruct((FIRST, 128), jnp.int32),
            jax.ShapeDtypeStruct((8, 2 * pairs.shape[0]), jnp.int32),
        ),
        in_specs=[SMEM] + [VMEM] * 3,
        out_specs=(VMEM,) * 3,
        compiler_params=pltpu.CompilerParams(vmem_limit_bytes=16 * MIB),
        cost_estimate=pl.CostEstimate(flops=10**9, bytes_accessed=10**6, transcendentals=0),
    )(me.reshape(1), pairs, lengths.reshape(1, -1), holder.reshape(1, -1))


def pick_kernel(selector, mine, picked, even, odd):
    rows, _, half = mine.shape

    @pl.when(pl.program_id(0) == 0)
    def _():
        units = mine[...].reshape(2 * rows, half)
        ends = units[:, 512:640].astype(F32)
        turned = half_turn(ends)
        low = iota(ends.shape, 1) < 64
        nil = jnp.zeros_like(ends)
        main = jnp.concatenate([units[:, 0:256], units[:, 256:512]], axis=0)
        first = jnp.concatenate([jnp.where(low, ends, nil), jnp.where(low, turned, nil)], axis=0)
        second = jnp.concatenate([jnp.where(low, nil, turned), jnp.where(low, nil, ends)], axis=0)
        even[...] = jnp.concatenate([main, first.astype(BF)], axis=1)
        odd[...] = jnp.concatenate([main, second.astype(BF)], axis=1)

    first = mm(selector[:, : 4 * rows], even[...])
    second = mm(selector[:, 4 * rows :], odd[...])
    rest = first[:, 256:] + second[:, 256:]
    message = jnp.concatenate([first[:, :256], second[:, :256], rest], axis=1).astype(BF)
    picked[...] = message.reshape(picked.shape)


def pick(selector, mine, outer):
    devices, _, half = mine.shape
    rows, units = selector.shape
    steps = 4
    nought = (0,) * (len(outer) + 1)
    return pl.pallas_call(
        pick_kernel,
        out_shape=jax.ShapeDtypeStruct((devices,) + outer + (half,), BF),
        grid=(steps,),
        in_specs=[
            pl.BlockSpec((rows // steps, units), lambda i: (i, 0)),
            pl.BlockSpec(mine.shape, lambda i: (0, 0, 0)),
        ],
        out_specs=pl.BlockSpec((devices // steps,) + outer + (half,), lambda i: (i,) + nought),
        scratch_shapes=[pltpu.VMEM((4 * devices, 384), BF)] * 2,
        compiler_params=pltpu.CompilerParams(vmem_limit_bytes=16 * MIB),
        cost_estimate=pl.CostEstimate(flops=10**9, bytes_accessed=10**7, transcendentals=0),
    )(selector, mine)


def query_kernel(own, other, weight, query):
    first = iota((128, 128), 0) < HEAD_DIM
    for who, rows in enumerate((own, other)):
        result = mm(rows[...], weight[...]).astype(BF).astype(F32) * HEAD_DIM**-0.5
        width = result.shape[1]
        for pair in range(width // 128):
            at = slice(who * width + pair * 128, who * width + (pair + 1) * 128)
            tile = jnp.transpose(result[:, pair * 128 : (pair + 1) * 128])
            query[at, :128] = jnp.where(first, tile, 0.0).astype(BF)
            query[at, 128:] = jnp.where(first, 0.0, tile).astype(BF)


def queries(own, other, weight):
    return pl.pallas_call(
        query_kernel,
        out_shape=jax.ShapeDtypeStruct((2 * own.shape[1], 256), BF),
        in_specs=[VMEM] * 3,
        out_specs=VMEM,
        compiler_params=pltpu.CompilerParams(vmem_limit_bytes=12 * MIB),
        cost_estimate=pl.CostEstimate(flops=10**9, bytes_accessed=10**7, transcendentals=0),
    )(own, other, weight)


def attend_kernel(
    meta, got_at, query_at, k_at, v_at, o_at, out, sibling,
    got, query, weight_k, weight_v, weight_o, rows, keys, values,
    context, scores, weights, scales, sems,
):
    copies = [
        pltpu.make_async_copy(a, b, sems.at[i])
        for i, (a, b) in enumerate(
            [(got_at, got), (k_at, weight_k), (v_at, weight_v), (query_at, query), (o_at, weight_o)]
        )
    ]
    for copy in copies[:3]:
        copy.start()
    width = weight_k.shape[0]
    each = 1
    for n in got.shape[1:-1]:
        each *= n
    tall = 16 * each
    context[...] = jnp.zeros_like(context)
    values[...] = jnp.zeros_like(values)
    lead, lane = iota((tall, tall), 0), iota((tall, tall), 1)
    n = jnp.int32(each)
    turned = (lead == lax.rem(lane, n) * 16 + lax.div(lane, n)).astype(BF)
    low = iota((tall, 128), 1) < 64
    copies[0].wait()
    copies[3].start()
    copies[4].start()
    for part in range(2):
        rests = []
        for quarter in range(4):
            at = quarter * BLOCK + part * 16
            piece = mm(turned, got[at : at + 16].reshape(tall, width // 2))
            rests.append(piece[:, 512:640])
            piece = piece.astype(BF)
            for u in range(2 * each):
                to = u * BLOCK + part * 16
                side = (u % 2) * 256
                rows[to : to + 16, quarter * 256 : quarter * 256 + 256] = piece[
                    (u // 2) * 16 : (u // 2) * 16 + 16, side : side + 256
                ]
            if quarter % 2 == 1:
                left, right = rests[-2:]
                even = jnp.where(low, left, half_turn(right)).astype(BF)
                odd = jnp.where(low, half_turn(left), right).astype(BF)
                tile = 1024 + 128 * (quarter // 2)
                for u in range(2 * each):
                    to = u * BLOCK + part * 16
                    rows[to : to + 16, tile : tile + 128] = (odd if u % 2 else even)[
                        (u // 2) * 16 : (u // 2) * 16 + 16
                    ]
    chunks = (meta[0, 7] + 7) // 8

    def project(weight, to):
        def some(chunk, carry):
            at = pl.ds(pl.multiple_of(chunk * 256, 256), 256)
            to[at, :] = mm(rows[at, :], weight[...]).astype(BF)
            return carry

        lax.fori_loop(0, chunks, some, 0)

    copies[1].wait()
    project(weight_k, keys)
    copies[2].wait()
    project(weight_v, values)
    copies[3].wait()

    def item(index, carry):
        start = pl.multiple_of(meta[index, 0] * BLOCK, BLOCK)
        length = meta[index, 1]
        whose = meta[index, 2]

        def with_keys(size):
            live = iota((size, 256), 0) < length
            span = pl.ds(start, size)
            pairs = range(width // 128)
            for pair in pairs:
                at = slice(pair * 128, (pair + 1) * 128)
                q = query[pl.ds(pl.multiple_of(whose * width + pair * 128, 128), 128), :]
                scores[:size, pair * 256 : (pair + 1) * 256] = mm(keys[span, at], q)
            for pair in pairs:
                at = slice(pair * 256, (pair + 1) * 256)
                score = jnp.where(live, scores[:size, at], -1e30)
                power = jnp.exp(score - jnp.max(score, axis=0, keepdims=True))
                weights[:size, at] = power.astype(BF)
                scales[0:1, at] = 1.0 / jnp.sum(power, axis=0, keepdims=True)
            for pair in pairs:
                at = slice(pair * 256, (pair + 1) * 256)
                v = values[span, pair * 128 : (pair + 1) * 128]
                result = lax.dot_general(v, weights[:size, at], DOWN, preferred_element_type=F32)
                scale = scales[0:1, at]
                to = pl.multiple_of(whose * width + pair * 128, 128)
                context[pl.ds(to, 64), :] += result[:64, :128] * scale[:, :128]
                context[pl.ds(to + 64, 64), :] += result[64:, 128:] * scale[:, 128:]

        @pl.when(length <= 64)
        def _():
            with_keys(64)

        @pl.when(length > 64)
        def _():
            with_keys(128)

        return carry

    lax.fori_loop(0, meta[0, 3], item, 0)
    copies[4].wait()
    for who, to in enumerate((out, sibling)):
        part = context[who * width : (who + 1) * width, :].astype(BF)
        update = lax.dot_general(part, weight_o[...], DOWN, preferred_element_type=F32)
        update = jnp.where(iota(update.shape, 0) < meta[0, 4 + who], update, 0.0)
        to[...] = update.astype(to.dtype)


def attend(meta, got, query, weight_k, weight_v, weight_o):
    width = weight_k.shape[0]
    each = 1
    for n in got.shape[1:-1]:
        each *= n
    tall = 2 * each * BLOCK
    return pl.pallas_call(
        attend_kernel,
        out_shape=(
            jax.ShapeDtypeStruct((128, width), F32),
            jax.ShapeDtypeStruct((128, width), BF),
        ),
        in_specs=[SMEM] + [ANY] * 5,
        out_specs=(VMEM, VMEM),
        scratch_shapes=[
            pltpu.VMEM(got.shape, BF),
            pltpu.VMEM(query.shape, BF),
            pltpu.VMEM((width, width), BF),
            pltpu.VMEM((width, width), BF),
            pltpu.VMEM((width, width), BF),
            pltpu.VMEM((tall, width), BF),
            pltpu.VMEM((tall + (PARTS - 1) * BLOCK, width), BF),
            pltpu.VMEM((tall + (PARTS - 1) * BLOCK, width), BF),
            pltpu.VMEM((2 * width, 128), F32),
            pltpu.VMEM((128, 2 * width), F32),
            pltpu.VMEM((128, 2 * width), BF),
            pltpu.VMEM((8, 2 * width), F32),
            pltpu.SemaphoreType.DMA((5,)),
        ],
        compiler_params=pltpu.CompilerParams(vmem_limit_bytes=36 * MIB),
        cost_estimate=pl.CostEstimate(flops=10**10, bytes_accessed=10**7, transcendentals=10**6),
    )(meta, got, query, weight_k, weight_v, weight_o)


def later_round(number, sides, me, count, meta):
    dest, source, length, amount, base, _, place, _ = sides
    origin = FIRST - PARTS + 1
    turn = jnp.where(base + amount <= FIRST, 0, 1 + (base - origin) // STEP)
    active = turn == number
    base = base - origin - (number - 1) * STEP
    spots = jnp.arange(LATER, dtype=jnp.int32)
    target = (dest[None, :] == jnp.arange(count, dtype=jnp.int32)[:, None]) & active[None, :]
    there = (base[:, None] <= spots) & (spots < (base + amount)[:, None])
    entries = [jnp.where(there, source[:, None] + 1, 0), jnp.where(there, spots - base[:, None], 0)]
    high, low = (mm(target.astype(BF), entry.astype(BF)).astype(jnp.int32) for entry in entries)
    unit = (4 * (high - 1) + low).reshape(-1, 2)
    columns = jnp.arange(4 * count, dtype=jnp.int32)
    unit_at = 2 * (columns % (2 * count)) + columns // (2 * count)
    selector = (unit[:, :, None] == unit_at).reshape(unit.shape[0], -1).astype(BF)
    held = active & (dest == me)
    order = jnp.cumsum(held.astype(jnp.int32)) - 1
    chosen = held[None, :] & (order[None, :] == spots[:, None])

    def listed(values):
        return jnp.sum(jnp.where(chosen, values[None, :], 0), axis=1)

    held_count = jnp.broadcast_to(jnp.sum(held.astype(jnp.int32)), (LATER,))
    columns = [listed(base), listed(length), listed((place + me) % 2), held_count]
    meta = meta[:LATER].at[:, :4].set(jnp.stack(columns, axis=1))
    return selector, meta.at[:, 7].set(jnp.max(jnp.where(held, base + amount, 0)))


def local(embeddings, weight_q, weight_k, weight_v, weight_o, pairs, lengths, holder):
    count = lax.axis_size("group") * lax.axis_size("dev")
    me = lax.axis_index("group") * lax.axis_size("dev") + lax.axis_index("dev")
    own = embeddings[0]
    mine = exchange(front(own))
    selector, meta, sides = plan(me, pairs, lengths, holder)
    rounds = meta[0, 6]
    query = queries(own, swap(own), weight_q)

    def one_round(selector, meta, outer):
        got = exchange(pick(selector, mine, outer))
        return attend(meta, got, query, weight_k, weight_v, weight_o)

    def another(carry):
        number, total = carry
        kept, given = one_round(*later_round(number, sides, me, count, meta), (LATER // 2,))
        return number + 1, total + kept + swap(given).astype(F32)

    kept, given = one_round(selector, meta, (FIRST // 8, 4))
    received = swap(given)
    _, kept = lax.while_loop(lambda c: c[0] <= rounds, another, (jnp.int32(1), kept))
    return (own.astype(F32) + (kept + received.astype(F32))).astype(BF)[None]


def solution(mesh):
    in_specs = (P(AXES, None, None), P(), P(), P(), P(), P(), P(), P())
    out_specs = P(AXES, None, None)
    return jax.shard_map(local, mesh=mesh, in_specs=in_specs, out_specs=out_specs, check_vma=False)
```

```python
import jax
import jax.numpy as jnp
from jax import lax
from jax.experimental import pallas as pl
from jax.experimental.pallas import tpu as pltpu
from jax.sharding import PartitionSpec as P

HEAD_DIM = 64
AXES = ("group", "dev")
BLOCK = 32
PARTS = 4
FIRST = 24
LATER = 16
STEP = LATER - PARTS + 1
MIB = 1024 * 1024
BF = jnp.bfloat16
F32 = jnp.float32
VMEM = pl.BlockSpec(memory_space=pltpu.VMEM)
SMEM = pl.BlockSpec(memory_space=pltpu.SMEM)
ANY = pl.BlockSpec(memory_space=pl.ANY)
ACROSS = (((1,), (1,)), ((), ()))
DOWN = (((0,), (0,)), ((), ()))


def exchange(array):
    return lax.all_to_all(array, AXES, split_axis=0, concat_axis=0, tiled=True)


def swap(array):
    count = lax.axis_size("dev")
    return lax.ppermute(array, "dev", [(i, i ^ 1) for i in range(count)])


def mm(a, b):
    return jnp.dot(a, b, preferred_element_type=F32)


def iota(shape, dim):
    return lax.broadcasted_iota(jnp.int32, shape, dim)


def half_turn(array):
    return pltpu.roll(array.astype(F32), 64, 1)


def front_kernel(own, pieces):
    low = iota((BLOCK, 128), 1) < 64
    for quarter in range(4):
        main = slice(256 * quarter, 256 * quarter + 256)
        tile = slice(1024 + 128 * (quarter // 2), 1152 + 128 * (quarter // 2))
        for h in range(2):
            even = slice(2 * h * BLOCK, (2 * h + 1) * BLOCK)
            odd = slice((2 * h + 1) * BLOCK, (2 * h + 2) * BLOCK)
            if quarter % 2 == 0:
                rest = jnp.where(low, own[even, tile].astype(F32), half_turn(own[odd, tile]))
            else:
                rest = jnp.where(low, half_turn(own[even, tile]), own[odd, tile].astype(F32))
            to = slice(quarter * BLOCK, (quarter + 1) * BLOCK)
            pieces[to, h, 0:256] = own[even, main]
            pieces[to, h, 256:512] = own[odd, main]
            pieces[to, h, 512:640] = rest.astype(BF)


def front(own):
    rows, width = own.shape
    return pl.pallas_call(
        front_kernel,
        out_shape=jax.ShapeDtypeStruct((rows, 2, width // 2), BF),
        in_specs=[VMEM],
        out_specs=VMEM,
        compiler_params=pltpu.CompilerParams(vmem_limit_bytes=4 * MIB),
    )(own)


def plan_kernel(place, pairs, lengths, holder, selector, meta, sides):
    me = place[0]
    count = pairs.shape[0]
    total = 2 * count
    devices = holder.shape[1]
    lane = iota((count, devices), 1)
    marks = [pairs[:, i : i + 1] == lane for i in range(2)]
    held_at = holder[...].astype(F32)
    long = lengths[...].astype(F32)
    places = [jnp.sum(jnp.where(m, held_at, 0.0), axis=1, keepdims=True) for m in marks]
    sizes = [jnp.sum(jnp.where(m, long, 0.0), axis=1, keepdims=True) for m in marks]
    place_col = jnp.concatenate(places, axis=0)
    source_col = jnp.concatenate(places[::-1], axis=0)
    length_col = jnp.concatenate(sizes[::-1], axis=0)
    lane = iota((total, devices), 1)
    listed = jnp.where(lane == 0, place_col, jnp.where(lane == 1, source_col, length_col))
    turned = jnp.transpose(listed).astype(jnp.int32)
    place_row, source, length = turned[0:1], turned[1:2], turned[2:3]
    amount = (length + (BLOCK - 1)) // BLOCK
    amount_col = ((length_col.astype(jnp.int32) + (BLOCK - 1)) // BLOCK).astype(F32)
    chip = place_row // 2
    tied = (amount_col == amount.astype(F32)) & (iota((total, total), 0) < iota((total, total), 1))
    earlier = (amount_col > amount.astype(F32)) | tied
    same = place_col.astype(jnp.int32) // 2 == chip
    before = jnp.sum(jnp.where(same & earlier, 1.0, 0.0), axis=0, keepdims=True).astype(jnp.int32)
    dest = 2 * chip + ((before + 1) // 2) % 2
    dest_col = jnp.transpose(jnp.broadcast_to(dest.astype(F32), (devices, total)))[:, 0:1]
    alike = (dest_col.astype(jnp.int32) == dest) & earlier
    base = jnp.sum(jnp.where(alike, amount_col, 0.0), axis=0, keepdims=True).astype(jnp.int32)
    slot = jnp.sum(jnp.where(alike, 1.0, 0.0), axis=0, keepdims=True).astype(jnp.int32)
    sides[...] = jnp.concatenate(
        [dest, source, length, amount, base, slot, place_row, place_row], axis=0
    )
    active = base + amount <= FIRST
    spot = iota((devices, total), 0)
    target = jnp.where((dest == spot) & active, 1.0, 0.0).astype(BF)
    there = (base <= spot) & (spot < base + amount)
    entry = jnp.where(there, source + 1, 0)
    shifted = spot - 64
    entry = entry + jnp.where((base <= shifted) & (shifted < base + amount), shifted - base, 0)
    table = lax.dot_general(target, entry.astype(F32).astype(BF), ACROSS, preferred_element_type=F32)
    rows = devices * FIRST // 2
    row, lane = iota((rows, devices), 0), iota((rows, devices), 1)
    which, v = lax.div(row, jnp.int32(FIRST // 2)), lax.rem(row, jnp.int32(FIRST // 2))
    spread = mm(jnp.where(which == lane, 1.0, 0.0).astype(BF), table.astype(BF))
    columns = iota((rows, 4 * devices), 1)
    unit_at = 2 * (columns % (2 * devices)) + columns // (2 * devices)
    for side in range(2):
        u = 2 * v + side
        value = jnp.where(lane == u, 4.0 * spread, jnp.where(lane == u + 64, spread, 0.0))
        unit = jnp.sum(value, axis=1, keepdims=True).astype(jnp.int32) - 4
        at = slice(side * 4 * devices, (side + 1) * 4 * devices)
        selector[:, at] = jnp.where(unit == unit_at, 1.0, 0.0).astype(BF)
    held = active & (dest == me)
    chosen = held & (slot == iota((FIRST, total), 0))

    def column(values):
        return jnp.sum(jnp.where(chosen, values.astype(F32), 0.0), axis=1, keepdims=True)

    amount_held = jnp.sum(jnp.where(held, 1.0, 0.0), axis=1, keepdims=True)
    rounds = jnp.max(jnp.where(active, 0, 1 + (base - (FIRST - PARTS + 1)) // STEP), axis=1, keepdims=True)
    ends = [
        jnp.sum(jnp.where(holder[...] == which, long, 0.0), axis=1, keepdims=True)
        for which in (me, me + 1 - 2 * (me % 2))
    ]
    lane = iota(meta.shape, 1)
    listed = jnp.where(lane == 1, column(length), column(base))
    listed = jnp.where(lane == 2, column((place_row + me) % 2), listed)
    listed = jnp.where(lane == 3, amount_held, listed)
    blocks = jnp.max(jnp.where(held, base + amount, 0), axis=1, keepdims=True).astype(F32)
    listed = jnp.where(lane == 7, blocks, listed)
    listed = jnp.where(lane == 4, ends[0], jnp.where(lane == 5, ends[1], listed))
    meta[...] = jnp.where(lane == 6, rounds.astype(F32), listed).astype(jnp.int32)


def plan(me, pairs, lengths, holder):
    devices = holder.shape[0]
    return pl.pallas_call(
        plan_kernel,
        out_shape=(
            jax.ShapeDtypeStruct((devices * FIRST // 2, 8 * devices), BF),
            jax.ShapeDtypeStruct((FIRST, 128), jnp.int32),
            jax.ShapeDtypeStruct((8, 2 * pairs.shape[0]), jnp.int32),
        ),
        in_specs=[SMEM] + [VMEM] * 3,
        out_specs=(VMEM,) * 3,
        compiler_params=pltpu.CompilerParams(vmem_limit_bytes=16 * MIB),
        cost_estimate=pl.CostEstimate(flops=10**9, bytes_accessed=10**6, transcendentals=0),
    )(me.reshape(1), pairs, lengths.reshape(1, -1), holder.reshape(1, -1))


def pick_kernel(selector, mine, picked, even, odd):
    rows, _, half = mine.shape

    @pl.when(pl.program_id(0) == 0)
    def _():
        units = mine[...].reshape(2 * rows, half)
        ends = units[:, 512:640].astype(F32)
        turned = half_turn(ends)
        low = iota(ends.shape, 1) < 64
        nil = jnp.zeros_like(ends)
        main = jnp.concatenate([units[:, 0:256], units[:, 256:512]], axis=0)
        first = jnp.concatenate([jnp.where(low, ends, nil), jnp.where(low, turned, nil)], axis=0)
        second = jnp.concatenate([jnp.where(low, nil, turned), jnp.where(low, nil, ends)], axis=0)
        even[...] = jnp.concatenate([main, first.astype(BF)], axis=1)
        odd[...] = jnp.concatenate([main, second.astype(BF)], axis=1)

    first = mm(selector[:, : 4 * rows], even[...])
    second = mm(selector[:, 4 * rows :], odd[...])
    rest = first[:, 256:] + second[:, 256:]
    message = jnp.concatenate([first[:, :256], second[:, :256], rest], axis=1).astype(BF)
    picked[...] = message.reshape(picked.shape)


def pick(selector, mine, outer):
    devices, _, half = mine.shape
    rows, units = selector.shape
    steps = 2
    nought = (0,) * (len(outer) + 1)
    return pl.pallas_call(
        pick_kernel,
        out_shape=jax.ShapeDtypeStruct((devices,) + outer + (half,), BF),
        grid=(steps,),
        in_specs=[
            pl.BlockSpec((rows // steps, units), lambda i: (i, 0)),
            pl.BlockSpec(mine.shape, lambda i: (0, 0, 0)),
        ],
        out_specs=pl.BlockSpec((devices // steps,) + outer + (half,), lambda i: (i,) + nought),
        scratch_shapes=[pltpu.VMEM((4 * devices, 384), BF)] * 2,
        compiler_params=pltpu.CompilerParams(vmem_limit_bytes=16 * MIB),
        cost_estimate=pl.CostEstimate(flops=10**9, bytes_accessed=10**7, transcendentals=0),
    )(selector, mine)


def query_kernel(own, other, weight, query):
    first = iota((128, 128), 0) < HEAD_DIM
    for who, rows in enumerate((own, other)):
        result = mm(rows[...], weight[...]).astype(BF).astype(F32) * HEAD_DIM**-0.5
        width = result.shape[1]
        for pair in range(width // 128):
            at = slice(who * width + pair * 128, who * width + (pair + 1) * 128)
            tile = jnp.transpose(result[:, pair * 128 : (pair + 1) * 128])
            query[at, :128] = jnp.where(first, tile, 0.0).astype(BF)
            query[at, 128:] = jnp.where(first, 0.0, tile).astype(BF)


def queries(own, other, weight):
    return pl.pallas_call(
        query_kernel,
        out_shape=jax.ShapeDtypeStruct((2 * own.shape[1], 256), BF),
        in_specs=[VMEM] * 3,
        out_specs=VMEM,
        compiler_params=pltpu.CompilerParams(vmem_limit_bytes=12 * MIB),
        cost_estimate=pl.CostEstimate(flops=10**9, bytes_accessed=10**7, transcendentals=0),
    )(own, other, weight)


def attend_kernel(
    meta, got_at, query_at, k_at, v_at, o_at, out, sibling,
    got, query, weight_k, weight_v, weight_o, rows, keys, values,
    context, scores, weights, scales, sems,
):
    copies = [
        pltpu.make_async_copy(a, b, sems.at[i])
        for i, (a, b) in enumerate(
            [(got_at, got), (k_at, weight_k), (v_at, weight_v), (query_at, query), (o_at, weight_o)]
        )
    ]
    for copy in copies[:3]:
        copy.start()
    width = weight_k.shape[0]
    each = 1
    for n in got.shape[1:-1]:
        each *= n
    tall = 16 * each
    context[...] = jnp.zeros_like(context)
    values[...] = jnp.zeros_like(values)
    lead, lane = iota((tall, tall), 0), iota((tall, tall), 1)
    n = jnp.int32(each)
    turned = (lead == lax.rem(lane, n) * 16 + lax.div(lane, n)).astype(BF)
    low = iota((tall, 128), 1) < 64
    copies[0].wait()
    copies[3].start()
    copies[4].start()
    for part in range(2):
        rests = []
        for quarter in range(4):
            at = quarter * BLOCK + part * 16
            piece = mm(turned, got[at : at + 16].reshape(tall, width // 2))
            rests.append(piece[:, 512:640])
            piece = piece.astype(BF)
            for u in range(2 * each):
                to = u * BLOCK + part * 16
                side = (u % 2) * 256
                rows[to : to + 16, quarter * 256 : quarter * 256 + 256] = piece[
                    (u // 2) * 16 : (u // 2) * 16 + 16, side : side + 256
                ]
            if quarter % 2 == 1:
                left, right = rests[-2:]
                even = jnp.where(low, left, half_turn(right)).astype(BF)
                odd = jnp.where(low, half_turn(left), right).astype(BF)
                tile = 1024 + 128 * (quarter // 2)
                for u in range(2 * each):
                    to = u * BLOCK + part * 16
                    rows[to : to + 16, tile : tile + 128] = (odd if u % 2 else even)[
                        (u // 2) * 16 : (u // 2) * 16 + 16
                    ]
    chunks = (meta[0, 7] + 7) // 8

    def project(weight, to):
        def some(chunk, carry):
            at = pl.ds(pl.multiple_of(chunk * 256, 256), 256)
            to[at, :] = mm(rows[at, :], weight[...]).astype(BF)
            return carry

        lax.fori_loop(0, chunks, some, 0)

    copies[1].wait()
    project(weight_k, keys)
    copies[2].wait()
    project(weight_v, values)
    copies[3].wait()

    def two_sides(index, carry):
        sides = [2 * index, 2 * index + 1]
        starts = [pl.multiple_of(meta[i, 0] * BLOCK, BLOCK) for i in sides]
        lengths = [meta[i, 1] for i in sides]
        whose = [meta[i, 2] for i in sides]
        pairs = range(width // 128)

        def with_keys(*sizes):
            positions = [iota((size, 256), 0) for size in sizes]

            def score(side, pair):
                at = slice(pair * 128, (pair + 1) * 128)
                first = pl.multiple_of(whose[side] * width + pair * 128, 128)
                size = sizes[side]
                result = mm(keys[pl.ds(starts[side], size), at], query[pl.ds(first, 128), :])
                scores[side, :size, pair * 256 : (pair + 1) * 256] = result

            def soften(side, pair):
                at = slice(pair * 256, (pair + 1) * 256)
                size = sizes[side]
                live = positions[side] < lengths[side]
                score = jnp.where(live, scores[side, :size, at], -1e30)
                power = jnp.exp(score - jnp.max(score, axis=0, keepdims=True))
                weights[side, :size, at] = power.astype(BF)
                scale = 1.0 / jnp.sum(power, axis=0, keepdims=True)
                scales[side, 0:1, at] = jnp.where(lengths[side] > 0, scale, 0.0)

            def gather(side, pair):
                at = slice(pair * 256, (pair + 1) * 256)
                size = sizes[side]
                v = values[pl.ds(starts[side], size), pair * 128 : (pair + 1) * 128]
                w = weights[side, :size, at]
                result = lax.dot_general(v, w, DOWN, preferred_element_type=F32)
                scale = scales[side, 0:1, at]
                to = pl.multiple_of(whose[side] * width + pair * 128, 128)
                context[pl.ds(to, 64), :] += result[:64, :128] * scale[:, :128]
                context[pl.ds(to + 64, 64), :] += result[64:, 128:] * scale[:, 128:]

            for pair in pairs:
                score(0, pair)
            for pair in pairs:
                score(1, pair)
                soften(0, pair)
            for pair in pairs:
                soften(1, pair)
                gather(0, pair)
            for pair in pairs:
                gather(1, pair)

        longer = [length > 64 for length in lengths]

        @pl.when(longer[1])
        def _():
            with_keys(128, 128)

        @pl.when(jnp.logical_and(longer[0], jnp.logical_not(longer[1])))
        def _():
            with_keys(128, 64)

        @pl.when(jnp.logical_not(jnp.logical_or(longer[0], longer[1])))
        def _():
            with_keys(64, 64)

        return carry

    lax.fori_loop(0, (meta[0, 3] + 1) // 2, two_sides, 0)
    copies[4].wait()
    for who, to in ((1, sibling), (0, out)):
        part = context[who * width : (who + 1) * width, :].astype(BF)
        update = lax.dot_general(part, weight_o[...], DOWN, preferred_element_type=F32)
        update = jnp.where(iota(update.shape, 0) < meta[0, 4 + who], update, 0.0)
        to[...] = update.astype(to.dtype)


def attend(meta, got, query, weight_k, weight_v, weight_o):
    width = weight_k.shape[0]
    each = 1
    for n in got.shape[1:-1]:
        each *= n
    tall = 2 * each * BLOCK
    return pl.pallas_call(
        attend_kernel,
        out_shape=(
            jax.ShapeDtypeStruct((128, width), F32),
            jax.ShapeDtypeStruct((128, width), BF),
        ),
        in_specs=[SMEM] + [ANY] * 5,
        out_specs=(VMEM, VMEM),
        scratch_shapes=[
            pltpu.VMEM(got.shape, BF),
            pltpu.VMEM(query.shape, BF),
            pltpu.VMEM((width, width), BF),
            pltpu.VMEM((width, width), BF),
            pltpu.VMEM((width, width), BF),
            pltpu.VMEM((tall, width), BF),
            pltpu.VMEM((tall + (PARTS - 1) * BLOCK, width), BF),
            pltpu.VMEM((tall + (PARTS - 1) * BLOCK, width), BF),
            pltpu.VMEM((2 * width, 128), F32),
            pltpu.VMEM((2, 128, 2 * width), F32),
            pltpu.VMEM((2, 128, 2 * width), BF),
            pltpu.VMEM((2, 8, 2 * width), F32),
            pltpu.SemaphoreType.DMA((5,)),
        ],
        compiler_params=pltpu.CompilerParams(vmem_limit_bytes=36 * MIB),
        cost_estimate=pl.CostEstimate(flops=10**10, bytes_accessed=10**7, transcendentals=10**6),
    )(meta, got, query, weight_k, weight_v, weight_o)


def later_round(number, sides, me, count, meta):
    dest, source, length, amount, base, _, place, _ = sides
    origin = FIRST - PARTS + 1
    turn = jnp.where(base + amount <= FIRST, 0, 1 + (base - origin) // STEP)
    active = turn == number
    base = base - origin - (number - 1) * STEP
    spots = jnp.arange(LATER, dtype=jnp.int32)
    target = (dest[None, :] == jnp.arange(count, dtype=jnp.int32)[:, None]) & active[None, :]
    there = (base[:, None] <= spots) & (spots < (base + amount)[:, None])
    entries = [jnp.where(there, source[:, None] + 1, 0), jnp.where(there, spots - base[:, None], 0)]
    high, low = (mm(target.astype(BF), entry.astype(BF)).astype(jnp.int32) for entry in entries)
    unit = (4 * (high - 1) + low).reshape(-1, 2)
    columns = jnp.arange(4 * count, dtype=jnp.int32)
    unit_at = 2 * (columns % (2 * count)) + columns // (2 * count)
    selector = (unit[:, :, None] == unit_at).reshape(unit.shape[0], -1).astype(BF)
    held = active & (dest == me)
    order = jnp.sum(held[:, None] & (base[:, None] < base[None, :]), axis=0)
    chosen = held[None, :] & (order[None, :] == spots[:, None])

    def listed(values):
        return jnp.sum(jnp.where(chosen, values[None, :], 0), axis=1)

    held_count = jnp.broadcast_to(jnp.sum(held.astype(jnp.int32)), (LATER,))
    columns = [listed(base), listed(length), listed((place + me) % 2), held_count]
    meta = meta[:LATER].at[:, :4].set(jnp.stack(columns, axis=1))
    return selector, meta.at[:, 7].set(jnp.max(jnp.where(held, base + amount, 0)))


def local(embeddings, weight_q, weight_k, weight_v, weight_o, pairs, lengths, holder):
    count = lax.axis_size("group") * lax.axis_size("dev")
    me = lax.axis_index("group") * lax.axis_size("dev") + lax.axis_index("dev")
    own = embeddings[0]
    mine = exchange(front(own))
    selector, meta, sides = plan(me, pairs, lengths, holder)
    rounds = meta[0, 6]
    query = queries(own, swap(own), weight_q)

    def one_round(selector, meta, outer):
        got = exchange(pick(selector, mine, outer))
        return attend(meta, got, query, weight_k, weight_v, weight_o)

    def another(carry):
        number, total = carry
        kept, given = one_round(*later_round(number, sides, me, count, meta), (LATER // 2,))
        return number + 1, total + kept + swap(given).astype(F32)

    kept, given = one_round(selector, meta, (FIRST // 8, 4))
    received = swap(given)
    _, kept = lax.while_loop(lambda c: c[0] <= rounds, another, (jnp.int32(1), kept))
    return (own.astype(F32) + (kept + received.astype(F32))).astype(BF)[None]


def solution(mesh):
    in_specs = (P(AXES, None, None), P(), P(), P(), P(), P(), P(), P())
    out_specs = P(AXES, None, None)
    return jax.shard_map(local, mesh=mesh, in_specs=in_specs, out_specs=out_specs, check_vma=False)
```

```python
import jax
import jax.numpy as jnp
from jax import lax
from jax.experimental import pallas as pl
from jax.experimental.pallas import tpu as pltpu
from jax.sharding import PartitionSpec as P

HEAD_DIM = 64
AXES = ("group", "dev")
BLOCK = 32
PARTS = 4
FIRST = 24
LATER = 16
STEP = LATER - PARTS + 1
MIB = 1024 * 1024
BF = jnp.bfloat16
F32 = jnp.float32
VMEM = pl.BlockSpec(memory_space=pltpu.VMEM)
SMEM = pl.BlockSpec(memory_space=pltpu.SMEM)
ANY = pl.BlockSpec(memory_space=pl.ANY)
ACROSS = (((1,), (1,)), ((), ()))
DOWN = (((0,), (0,)), ((), ()))


def exchange(array):
    return lax.all_to_all(array, AXES, split_axis=0, concat_axis=0, tiled=True)


def swap(array):
    count = lax.axis_size("dev")
    return lax.ppermute(array, "dev", [(i, i ^ 1) for i in range(count)])


def mm(a, b):
    return jnp.dot(a, b, preferred_element_type=F32)


def iota(shape, dim):
    return lax.broadcasted_iota(jnp.int32, shape, dim)


def half_turn(array):
    return pltpu.roll(array.astype(F32), 64, 1)


def front_kernel(own, pieces):
    low = iota((BLOCK, 128), 1) < 64
    for quarter in range(4):
        main = slice(256 * quarter, 256 * quarter + 256)
        tile = slice(1024 + 128 * (quarter // 2), 1152 + 128 * (quarter // 2))
        for h in range(2):
            even = slice(2 * h * BLOCK, (2 * h + 1) * BLOCK)
            odd = slice((2 * h + 1) * BLOCK, (2 * h + 2) * BLOCK)
            if quarter % 2 == 0:
                rest = jnp.where(low, own[even, tile].astype(F32), half_turn(own[odd, tile]))
            else:
                rest = jnp.where(low, half_turn(own[even, tile]), own[odd, tile].astype(F32))
            to = slice(quarter * BLOCK, (quarter + 1) * BLOCK)
            pieces[to, h, 0:256] = own[even, main]
            pieces[to, h, 256:512] = own[odd, main]
            pieces[to, h, 512:640] = rest.astype(BF)


def front(own):
    rows, width = own.shape
    return pl.pallas_call(
        front_kernel,
        out_shape=jax.ShapeDtypeStruct((rows, 2, width // 2), BF),
        in_specs=[VMEM],
        out_specs=VMEM,
        compiler_params=pltpu.CompilerParams(vmem_limit_bytes=4 * MIB),
    )(own)


def plan_kernel(place, pairs, lengths, holder, selector, meta, sides):
    me = place[0]
    count = pairs.shape[0]
    total = 2 * count
    devices = holder.shape[1]
    lane = iota((count, devices), 1)
    marks = [pairs[:, i : i + 1] == lane for i in range(2)]
    held_at = holder[...].astype(F32)
    long = lengths[...].astype(F32)
    places = [jnp.sum(jnp.where(m, held_at, 0.0), axis=1, keepdims=True) for m in marks]
    sizes = [jnp.sum(jnp.where(m, long, 0.0), axis=1, keepdims=True) for m in marks]
    place_col = jnp.concatenate(places, axis=0)
    source_col = jnp.concatenate(places[::-1], axis=0)
    length_col = jnp.concatenate(sizes[::-1], axis=0)
    lane = iota((total, devices), 1)
    listed = jnp.where(lane == 0, place_col, jnp.where(lane == 1, source_col, length_col))
    turned = jnp.transpose(listed).astype(jnp.int32)
    place_row, source, length = turned[0:1], turned[1:2], turned[2:3]
    amount = (length + (BLOCK - 1)) // BLOCK
    amount_col = ((length_col.astype(jnp.int32) + (BLOCK - 1)) // BLOCK).astype(F32)
    chip = place_row // 2
    tied = (amount_col == amount.astype(F32)) & (iota((total, total), 0) < iota((total, total), 1))
    earlier = (amount_col > amount.astype(F32)) | tied
    same = place_col.astype(jnp.int32) // 2 == chip
    before = jnp.sum(jnp.where(same & earlier, 1.0, 0.0), axis=0, keepdims=True).astype(jnp.int32)
    dest = 2 * chip + ((before + 1) // 2) % 2
    dest_col = jnp.transpose(jnp.broadcast_to(dest.astype(F32), (devices, total)))[:, 0:1]
    alike = (dest_col.astype(jnp.int32) == dest) & earlier
    base = jnp.sum(jnp.where(alike, amount_col, 0.0), axis=0, keepdims=True).astype(jnp.int32)
    slot = jnp.sum(jnp.where(alike, 1.0, 0.0), axis=0, keepdims=True).astype(jnp.int32)
    sides[...] = jnp.concatenate(
        [dest, source, length, amount, base, slot, place_row, place_row], axis=0
    )
    active = base + amount <= FIRST
    spot = iota((devices, total), 0)
    target = jnp.where((dest == spot) & active, 1.0, 0.0).astype(BF)
    there = (base <= spot) & (spot < base + amount)
    entry = jnp.where(there, source + 1, 0)
    shifted = spot - 64
    entry = entry + jnp.where((base <= shifted) & (shifted < base + amount), shifted - base, 0)
    table = lax.dot_general(target, entry.astype(F32).astype(BF), ACROSS, preferred_element_type=F32)
    rows = devices * FIRST // 2
    row, lane = iota((rows, devices), 0), iota((rows, devices), 1)
    which, v = lax.div(row, jnp.int32(FIRST // 2)), lax.rem(row, jnp.int32(FIRST // 2))
    spread = mm(jnp.where(which == lane, 1.0, 0.0).astype(BF), table.astype(BF))
    columns = iota((rows, 4 * devices), 1)
    unit_at = 2 * (columns % (2 * devices)) + columns // (2 * devices)
    for side in range(2):
        u = 2 * v + side
        value = jnp.where(lane == u, 4.0 * spread, jnp.where(lane == u + 64, spread, 0.0))
        unit = jnp.sum(value, axis=1, keepdims=True).astype(jnp.int32) - 4
        at = slice(side * 4 * devices, (side + 1) * 4 * devices)
        selector[:, at] = jnp.where(unit == unit_at, 1.0, 0.0).astype(BF)
    held = active & (dest == me)
    chosen = held & (slot == iota((FIRST, total), 0))

    def column(values):
        return jnp.sum(jnp.where(chosen, values.astype(F32), 0.0), axis=1, keepdims=True)

    amount_held = jnp.sum(jnp.where(held, 1.0, 0.0), axis=1, keepdims=True)
    rounds = jnp.max(jnp.where(active, 0, 1 + (base - (FIRST - PARTS + 1)) // STEP), axis=1, keepdims=True)
    ends = [
        jnp.sum(jnp.where(holder[...] == which, long, 0.0), axis=1, keepdims=True)
        for which in (me, me + 1 - 2 * (me % 2))
    ]
    lane = iota(meta.shape, 1)
    listed = jnp.where(lane == 1, column(length), column(base))
    listed = jnp.where(lane == 2, column((place_row + me) % 2), listed)
    listed = jnp.where(lane == 3, amount_held, listed)
    blocks = jnp.max(jnp.where(held, base + amount, 0), axis=1, keepdims=True).astype(F32)
    listed = jnp.where(lane == 7, blocks, listed)
    listed = jnp.where(lane == 4, ends[0], jnp.where(lane == 5, ends[1], listed))
    meta[...] = jnp.where(lane == 6, rounds.astype(F32), listed).astype(jnp.int32)


def plan(me, pairs, lengths, holder):
    devices = holder.shape[0]
    return pl.pallas_call(
        plan_kernel,
        out_shape=(
            jax.ShapeDtypeStruct((devices * FIRST // 2, 8 * devices), BF),
            jax.ShapeDtypeStruct((FIRST, 128), jnp.int32),
            jax.ShapeDtypeStruct((8, 2 * pairs.shape[0]), jnp.int32),
        ),
        in_specs=[SMEM] + [VMEM] * 3,
        out_specs=(VMEM,) * 3,
        compiler_params=pltpu.CompilerParams(vmem_limit_bytes=16 * MIB),
        cost_estimate=pl.CostEstimate(flops=10**9, bytes_accessed=10**6, transcendentals=0),
    )(me.reshape(1), pairs, lengths.reshape(1, -1), holder.reshape(1, -1))


def pick_kernel(selector_at, mine_at, picked_at, selector, mine, picked, even, odd, sems):
    rows, _, half = mine.shape
    pieces = 4
    tall, deep = selector.shape[0] // pieces, picked.shape[0] // pieces
    arrive = [pltpu.make_async_copy(mine_at, mine, sems.at[2 * pieces])]
    leave = []
    for i in range(pieces):
        at, to = pl.ds(i * tall, tall), pl.ds(i * deep, deep)
        arrive.append(pltpu.make_async_copy(selector_at.at[at], selector.at[at], sems.at[i]))
        leave.append(pltpu.make_async_copy(picked.at[to], picked_at.at[to], sems.at[pieces + i]))
    for copy in arrive:
        copy.start()
    arrive[0].wait()
    units = mine[...].reshape(2 * rows, half)
    ends = units[:, 512:640].astype(F32)
    turned = half_turn(ends)
    low = iota(ends.shape, 1) < 64
    nil = jnp.zeros_like(ends)
    main = jnp.concatenate([units[:, 0:256], units[:, 256:512]], axis=0)
    first = jnp.concatenate([jnp.where(low, ends, nil), jnp.where(low, turned, nil)], axis=0)
    second = jnp.concatenate([jnp.where(low, nil, turned), jnp.where(low, nil, ends)], axis=0)
    even[...] = jnp.concatenate([main, first.astype(BF)], axis=1)
    odd[...] = jnp.concatenate([main, second.astype(BF)], axis=1)
    for i in range(pieces):
        arrive[1 + i].wait()
        at, to = slice(i * tall, (i + 1) * tall), slice(i * deep, (i + 1) * deep)
        first = mm(selector[at, : 4 * rows], even[...])
        second = mm(selector[at, 4 * rows :], odd[...])
        rest = first[:, 256:] + second[:, 256:]
        message = jnp.concatenate([first[:, :256], second[:, :256], rest], axis=1).astype(BF)
        picked[to] = message.reshape((deep,) + picked.shape[1:])
        leave[i].start()
    for copy in leave:
        copy.wait()


def pick(selector, mine, outer):
    devices, _, half = mine.shape
    shape = (devices,) + outer + (half,)
    return pl.pallas_call(
        pick_kernel,
        out_shape=jax.ShapeDtypeStruct(shape, BF),
        in_specs=[ANY] * 2,
        out_specs=ANY,
        scratch_shapes=[
            pltpu.VMEM(selector.shape, BF),
            pltpu.VMEM(mine.shape, BF),
            pltpu.VMEM(shape, BF),
            pltpu.VMEM((4 * devices, 384), BF),
            pltpu.VMEM((4 * devices, 384), BF),
            pltpu.SemaphoreType.DMA((9,)),
        ],
        compiler_params=pltpu.CompilerParams(vmem_limit_bytes=16 * MIB),
        cost_estimate=pl.CostEstimate(flops=10**9, bytes_accessed=10**7, transcendentals=0),
    )(selector, mine)


def query_kernel(own, other, weight, query):
    first = iota((128, 128), 0) < HEAD_DIM
    for who, rows in enumerate((own, other)):
        result = mm(rows[...], weight[...]).astype(BF).astype(F32) * HEAD_DIM**-0.5
        width = result.shape[1]
        for pair in range(width // 128):
            at = slice(who * width + pair * 128, who * width + (pair + 1) * 128)
            tile = jnp.transpose(result[:, pair * 128 : (pair + 1) * 128])
            query[at, :128] = jnp.where(first, tile, 0.0).astype(BF)
            query[at, 128:] = jnp.where(first, 0.0, tile).astype(BF)


def queries(own, other, weight):
    return pl.pallas_call(
        query_kernel,
        out_shape=jax.ShapeDtypeStruct((2 * own.shape[1], 256), BF),
        in_specs=[VMEM] * 3,
        out_specs=VMEM,
        compiler_params=pltpu.CompilerParams(vmem_limit_bytes=12 * MIB),
        cost_estimate=pl.CostEstimate(flops=10**9, bytes_accessed=10**7, transcendentals=0),
    )(own, other, weight)


def attend_kernel(
    meta_at, got_at, query_at, k_at, v_at, o_at, out_at, sibling_at,
    meta, got, query, weight_k, weight_v, weight_o, rows, keys, values,
    context, scores, weights, scales, out, sibling, sems,
):
    def copy(index, source, target):
        return pltpu.make_async_copy(source, target, sems.at[index])

    quarters = []
    for quarter in range(4):
        at = pl.ds(quarter * BLOCK, BLOCK)
        quarters.append(copy(quarter, got_at.at[at], got.at[at]))
    copies = [
        copy(4 + i, a, b)
        for i, (a, b) in enumerate(
            [(meta_at, meta), (k_at, weight_k), (v_at, weight_v), (query_at, query), (o_at, weight_o)]
        )
    ]
    for one in quarters + copies[:3]:
        one.start()
    width = weight_k.shape[0]
    each = 1
    for n in got.shape[1:-1]:
        each *= n
    tall = 16 * each
    context[...] = jnp.zeros_like(context)
    values[...] = jnp.zeros_like(values)
    lead, lane = iota((tall, tall), 0), iota((tall, tall), 1)
    n = jnp.int32(each)
    turned = (lead == lax.rem(lane, n) * 16 + lax.div(lane, n)).astype(BF)
    low = iota((tall, 128), 1) < 64
    rests = {}
    for quarter in range(4):
        quarters[quarter].wait()
        for part in range(2):
            at = quarter * BLOCK + part * 16
            piece = mm(turned, got[at : at + 16].reshape(tall, width // 2))
            rests[quarter, part] = piece[:, 512:640]
            piece = piece.astype(BF)
            for u in range(2 * each):
                to = u * BLOCK + part * 16
                side = (u % 2) * 256
                rows[to : to + 16, quarter * 256 : quarter * 256 + 256] = piece[
                    (u // 2) * 16 : (u // 2) * 16 + 16, side : side + 256
                ]
            if quarter % 2 == 1:
                left, right = rests[quarter - 1, part], rests[quarter, part]
                even = jnp.where(low, left, half_turn(right)).astype(BF)
                odd = jnp.where(low, half_turn(left), right).astype(BF)
                tile = 1024 + 128 * (quarter // 2)
                for u in range(2 * each):
                    to = u * BLOCK + part * 16
                    rows[to : to + 16, tile : tile + 128] = (odd if u % 2 else even)[
                        (u // 2) * 16 : (u // 2) * 16 + 16
                    ]
    copies[3].start()
    copies[4].start()
    copies[0].wait()
    chunks = (meta[0, 7] + 7) // 8

    def project(weight, to):
        def some(chunk, carry):
            at = pl.ds(pl.multiple_of(chunk * 256, 256), 256)
            to[at, :] = mm(rows[at, :], weight[...]).astype(BF)
            return carry

        lax.fori_loop(0, chunks, some, 0)

    copies[1].wait()
    project(weight_k, keys)
    copies[2].wait()
    project(weight_v, values)
    copies[3].wait()

    def two_sides(index, carry):
        sides = [2 * index, 2 * index + 1]
        starts = [pl.multiple_of(meta[i, 0] * BLOCK, BLOCK) for i in sides]
        lengths = [meta[i, 1] for i in sides]
        whose = [meta[i, 2] for i in sides]
        pairs = range(width // 128)

        def with_keys(*sizes):
            positions = [iota((size, 256), 0) for size in sizes]

            def score(side, pair):
                at = slice(pair * 128, (pair + 1) * 128)
                first = pl.multiple_of(whose[side] * width + pair * 128, 128)
                size = sizes[side]
                result = mm(keys[pl.ds(starts[side], size), at], query[pl.ds(first, 128), :])
                scores[side, :size, pair * 256 : (pair + 1) * 256] = result

            def soften(side, pair):
                at = slice(pair * 256, (pair + 1) * 256)
                size = sizes[side]
                live = positions[side] < lengths[side]
                score = jnp.where(live, scores[side, :size, at], -1e30)
                power = jnp.exp(score - jnp.max(score, axis=0, keepdims=True))
                weights[side, :size, at] = power.astype(BF)
                scale = 1.0 / jnp.sum(power, axis=0, keepdims=True)
                scales[side, 0:1, at] = jnp.where(lengths[side] > 0, scale, 0.0)

            def gather(side, pair):
                at = slice(pair * 256, (pair + 1) * 256)
                size = sizes[side]
                v = values[pl.ds(starts[side], size), pair * 128 : (pair + 1) * 128]
                w = weights[side, :size, at]
                result = lax.dot_general(v, w, DOWN, preferred_element_type=F32)
                scale = scales[side, 0:1, at]
                to = pl.multiple_of(whose[side] * width + pair * 128, 128)
                context[pl.ds(to, 64), :] += result[:64, :128] * scale[:, :128]
                context[pl.ds(to + 64, 64), :] += result[64:, 128:] * scale[:, 128:]

            for pair in pairs:
                score(0, pair)
            for pair in pairs:
                score(1, pair)
                soften(0, pair)
            for pair in pairs:
                soften(1, pair)
                gather(0, pair)
            for pair in pairs:
                gather(1, pair)

        longer = [length > 64 for length in lengths]

        @pl.when(longer[1])
        def _():
            with_keys(128, 128)

        @pl.when(jnp.logical_and(longer[0], jnp.logical_not(longer[1])))
        def _():
            with_keys(128, 64)

        @pl.when(jnp.logical_not(jnp.logical_or(longer[0], longer[1])))
        def _():
            with_keys(64, 64)

        return carry

    lax.fori_loop(0, (meta[0, 3] + 1) // 2, two_sides, 0)
    copies[4].wait()
    part = context[width:, :].astype(BF)
    update = lax.dot_general(part, weight_o[...], DOWN, preferred_element_type=F32)
    sibling[...] = jnp.where(iota(update.shape, 0) < meta[0, 5], update, 0.0).astype(BF)
    leave = [copy(9, sibling, sibling_at)]
    leave[0].start()
    part = context[:width, :].astype(BF)
    for half in range(2):
        at = pl.ds(half * (width // 2), width // 2)
        update = lax.dot_general(part, weight_o[:, at], DOWN, preferred_element_type=F32)
        out[:, at] = jnp.where(iota(update.shape, 0) < meta[0, 4], update, 0.0)
        leave.append(copy(10 + half, out.at[:, at], out_at.at[:, at]))
        leave[-1].start()
    for one in leave:
        one.wait()


def attend(meta, got, query, weight_k, weight_v, weight_o):
    width = weight_k.shape[0]
    each = 1
    for n in got.shape[1:-1]:
        each *= n
    tall = 2 * each * BLOCK
    return pl.pallas_call(
        attend_kernel,
        out_shape=(
            jax.ShapeDtypeStruct((128, width), F32),
            jax.ShapeDtypeStruct((128, width), BF),
        ),
        in_specs=[ANY] * 6,
        out_specs=(ANY, ANY),
        scratch_shapes=[
            pltpu.SMEM(meta.shape, jnp.int32),
            pltpu.VMEM(got.shape, BF),
            pltpu.VMEM(query.shape, BF),
            pltpu.VMEM((width, width), BF),
            pltpu.VMEM((width, width), BF),
            pltpu.VMEM((width, width), BF),
            pltpu.VMEM((tall, width), BF),
            pltpu.VMEM((tall + (PARTS - 1) * BLOCK, width), BF),
            pltpu.VMEM((tall + (PARTS - 1) * BLOCK, width), BF),
            pltpu.VMEM((2 * width, 128), F32),
            pltpu.VMEM((2, 128, 2 * width), F32),
            pltpu.VMEM((2, 128, 2 * width), BF),
            pltpu.VMEM((2, 8, 2 * width), F32),
            pltpu.VMEM((128, width), F32),
            pltpu.VMEM((128, width), BF),
            pltpu.SemaphoreType.DMA((12,)),
        ],
        compiler_params=pltpu.CompilerParams(vmem_limit_bytes=36 * MIB),
        cost_estimate=pl.CostEstimate(flops=10**10, bytes_accessed=10**7, transcendentals=10**6),
    )(meta, got, query, weight_k, weight_v, weight_o)


def later_round(number, sides, me, count, meta):
    dest, source, length, amount, base, _, place, _ = sides
    origin = FIRST - PARTS + 1
    turn = jnp.where(base + amount <= FIRST, 0, 1 + (base - origin) // STEP)
    active = turn == number
    base = base - origin - (number - 1) * STEP
    spots = jnp.arange(LATER, dtype=jnp.int32)
    target = (dest[None, :] == jnp.arange(count, dtype=jnp.int32)[:, None]) & active[None, :]
    there = (base[:, None] <= spots) & (spots < (base + amount)[:, None])
    entries = [jnp.where(there, source[:, None] + 1, 0), jnp.where(there, spots - base[:, None], 0)]
    high, low = (mm(target.astype(BF), entry.astype(BF)).astype(jnp.int32) for entry in entries)
    unit = (4 * (high - 1) + low).reshape(-1, 2)
    columns = jnp.arange(4 * count, dtype=jnp.int32)
    unit_at = 2 * (columns % (2 * count)) + columns // (2 * count)
    selector = (unit[:, :, None] == unit_at).reshape(unit.shape[0], -1).astype(BF)
    held = active & (dest == me)
    order = jnp.sum(held[:, None] & (base[:, None] < base[None, :]), axis=0)
    chosen = held[None, :] & (order[None, :] == spots[:, None])

    def listed(values):
        return jnp.sum(jnp.where(chosen, values[None, :], 0), axis=1)

    held_count = jnp.broadcast_to(jnp.sum(held.astype(jnp.int32)), (LATER,))
    columns = [listed(base), listed(length), listed((place + me) % 2), held_count]
    meta = meta[:LATER].at[:, :4].set(jnp.stack(columns, axis=1))
    return selector, meta.at[:, 7].set(jnp.max(jnp.where(held, base + amount, 0)))


def local(embeddings, weight_q, weight_k, weight_v, weight_o, pairs, lengths, holder):
    count = lax.axis_size("group") * lax.axis_size("dev")
    me = lax.axis_index("group") * lax.axis_size("dev") + lax.axis_index("dev")
    own = embeddings[0]
    mine = exchange(front(own))
    selector, meta, sides = plan(me, pairs, lengths, holder)
    rounds = meta[0, 6]
    query = queries(own, swap(own), weight_q)

    def one_round(selector, meta, outer):
        got = exchange(pick(selector, mine, outer))
        return attend(meta, got, query, weight_k, weight_v, weight_o)

    def another(carry):
        number, total = carry
        kept, given = one_round(*later_round(number, sides, me, count, meta), (LATER // 2,))
        return number + 1, total + kept + swap(given).astype(F32)

    kept, given = one_round(selector, meta, (FIRST // 8, 4))
    received = swap(given)
    _, kept = lax.while_loop(lambda c: c[0] <= rounds, another, (jnp.int32(1), kept))
    return (own.astype(F32) + (kept + received.astype(F32))).astype(BF)[None]


def solution(mesh):
    in_specs = (P(AXES, None, None), P(), P(), P(), P(), P(), P(), P())
    out_specs = P(AXES, None, None)
    return jax.shard_map(local, mesh=mesh, in_specs=in_specs, out_specs=out_specs, check_vma=False)
```

```python
import jax
import jax.numpy as jnp
from jax import lax
from jax.experimental import pallas as pl
from jax.experimental.pallas import tpu as pltpu
from jax.sharding import PartitionSpec as P

HEAD_DIM = 64
AXES = ("group", "dev")
BLOCK = 32
PARTS = 4
FIRST = 24
LATER = 16
STEP = LATER - PARTS + 1
MIB = 1024 * 1024
BF = jnp.bfloat16
F32 = jnp.float32
VMEM = pl.BlockSpec(memory_space=pltpu.VMEM)
SMEM = pl.BlockSpec(memory_space=pltpu.SMEM)
ANY = pl.BlockSpec(memory_space=pl.ANY)
ACROSS = (((1,), (1,)), ((), ()))
DOWN = (((0,), (0,)), ((), ()))


def exchange(array):
    return lax.all_to_all(array, AXES, split_axis=0, concat_axis=0, tiled=True)


def swap(array):
    count = lax.axis_size("dev")
    return lax.ppermute(array, "dev", [(i, i ^ 1) for i in range(count)])


def mm(a, b):
    return jnp.dot(a, b, preferred_element_type=F32)


def iota(shape, dim):
    return lax.broadcasted_iota(jnp.int32, shape, dim)


def half_turn(array):
    return pltpu.roll(array.astype(F32), 64, 1)


def front_kernel(own_at, pieces_at, own, pieces, sems):
    low = iota((BLOCK, 128), 1) < 64
    arrive, leave = [], []
    for i in range(4):
        at = pl.ds(i * BLOCK, BLOCK)
        arrive.append(pltpu.make_async_copy(own_at.at[at], own.at[at], sems.at[i]))
        leave.append(pltpu.make_async_copy(pieces.at[at], pieces_at.at[at], sems.at[4 + i]))
    for copy in arrive:
        copy.start()
    for h in range(2):
        arrive[2 * h].wait()
        arrive[2 * h + 1].wait()
        even = slice(2 * h * BLOCK, (2 * h + 1) * BLOCK)
        odd = slice((2 * h + 1) * BLOCK, (2 * h + 2) * BLOCK)
        for quarter in range(4):
            main = slice(256 * quarter, 256 * quarter + 256)
            tile = slice(1024 + 128 * (quarter // 2), 1152 + 128 * (quarter // 2))
            if quarter % 2 == 0:
                rest = jnp.where(low, own[even, tile].astype(F32), half_turn(own[odd, tile]))
            else:
                rest = jnp.where(low, half_turn(own[even, tile]), own[odd, tile].astype(F32))
            to = slice(quarter * BLOCK, (quarter + 1) * BLOCK)
            pieces[to, h, 0:256] = own[even, main]
            pieces[to, h, 256:512] = own[odd, main]
            pieces[to, h, 512:640] = rest.astype(BF)
            if h == 1:
                leave[quarter].start()
    for copy in leave:
        copy.wait()


def front(own):
    rows, width = own.shape
    return pl.pallas_call(
        front_kernel,
        out_shape=jax.ShapeDtypeStruct((rows, 2, width // 2), BF),
        in_specs=[ANY],
        out_specs=ANY,
        scratch_shapes=[
            pltpu.VMEM((rows, width), BF),
            pltpu.VMEM((rows, 2, width // 2), BF),
            pltpu.SemaphoreType.DMA((8,)),
        ],
        compiler_params=pltpu.CompilerParams(vmem_limit_bytes=4 * MIB),
    )(own)


def plan_kernel(place, pairs, lengths, holder, selector, meta, sides):
    me = place[0]
    count = pairs.shape[0]
    total = 2 * count
    devices = holder.shape[1]
    lane = iota((count, devices), 1)
    marks = [pairs[:, i : i + 1] == lane for i in range(2)]
    held_at = holder[...].astype(F32)
    long = lengths[...].astype(F32)
    places = [jnp.sum(jnp.where(m, held_at, 0.0), axis=1, keepdims=True) for m in marks]
    sizes = [jnp.sum(jnp.where(m, long, 0.0), axis=1, keepdims=True) for m in marks]
    place_col = jnp.concatenate(places, axis=0)
    source_col = jnp.concatenate(places[::-1], axis=0)
    length_col = jnp.concatenate(sizes[::-1], axis=0)
    lane = iota((total, devices), 1)
    listed = jnp.where(lane == 0, place_col, jnp.where(lane == 1, source_col, length_col))
    turned = jnp.transpose(listed).astype(jnp.int32)
    place_row, source, length = turned[0:1], turned[1:2], turned[2:3]
    amount = (length + (BLOCK - 1)) // BLOCK
    amount_col = ((length_col.astype(jnp.int32) + (BLOCK - 1)) // BLOCK).astype(F32)
    chip = place_row // 2
    tied = (amount_col == amount.astype(F32)) & (iota((total, total), 0) < iota((total, total), 1))
    earlier = (amount_col > amount.astype(F32)) | tied
    same = place_col.astype(jnp.int32) // 2 == chip
    before = jnp.sum(jnp.where(same & earlier, 1.0, 0.0), axis=0, keepdims=True).astype(jnp.int32)
    dest = 2 * chip + ((before + 1) // 2) % 2
    dest_col = jnp.transpose(jnp.broadcast_to(dest.astype(F32), (devices, total)))[:, 0:1]
    alike = (dest_col.astype(jnp.int32) == dest) & earlier
    base = jnp.sum(jnp.where(alike, amount_col, 0.0), axis=0, keepdims=True).astype(jnp.int32)
    slot = jnp.sum(jnp.where(alike, 1.0, 0.0), axis=0, keepdims=True).astype(jnp.int32)
    sides[...] = jnp.concatenate(
        [dest, source, length, amount, base, slot, place_row, place_row], axis=0
    )
    active = base + amount <= FIRST
    spot = iota((devices, total), 0)
    target = jnp.where((dest == spot) & active, 1.0, 0.0).astype(BF)
    there = (base <= spot) & (spot < base + amount)
    entry = jnp.where(there, source + 1, 0)
    shifted = spot - 64
    entry = entry + jnp.where((base <= shifted) & (shifted < base + amount), shifted - base, 0)
    table = lax.dot_general(target, entry.astype(F32).astype(BF), ACROSS, preferred_element_type=F32)
    rows = devices * FIRST // 2
    row, lane = iota((rows, devices), 0), iota((rows, devices), 1)
    which, v = lax.div(row, jnp.int32(FIRST // 2)), lax.rem(row, jnp.int32(FIRST // 2))
    spread = mm(jnp.where(which == lane, 1.0, 0.0).astype(BF), table.astype(BF))
    columns = iota((rows, 2 * devices), 1)
    for side in range(2):
        u = 2 * v + side
        value = jnp.where(lane == u, 4.0 * spread, jnp.where(lane == u + 64, spread, 0.0))
        unit = jnp.sum(value, axis=1, keepdims=True).astype(jnp.int32) - 4
        sign = (1 - 2 * (unit % 2)).astype(F32)
        at = slice(side * 2 * devices, (side + 1) * 2 * devices)
        selector[:, at] = jnp.where(unit // 2 == columns, sign, 0.0).astype(BF)
    held = active & (dest == me)
    chosen = held & (slot == iota((FIRST, total), 0))

    def column(values):
        return jnp.sum(jnp.where(chosen, values.astype(F32), 0.0), axis=1, keepdims=True)

    amount_held = jnp.sum(jnp.where(held, 1.0, 0.0), axis=1, keepdims=True)
    rounds = jnp.max(jnp.where(active, 0, 1 + (base - (FIRST - PARTS + 1)) // STEP), axis=1, keepdims=True)
    ends = [
        jnp.sum(jnp.where(holder[...] == which, long, 0.0), axis=1, keepdims=True)
        for which in (me, me + 1 - 2 * (me % 2))
    ]
    lane = iota(meta.shape, 1)
    listed = jnp.where(lane == 1, column(length), column(base))
    listed = jnp.where(lane == 2, column((place_row + me) % 2), listed)
    listed = jnp.where(lane == 3, amount_held, listed)
    blocks = jnp.max(jnp.where(held, base + amount, 0), axis=1, keepdims=True).astype(F32)
    listed = jnp.where(lane == 7, blocks, listed)
    listed = jnp.where(lane == 4, ends[0], jnp.where(lane == 5, ends[1], listed))
    meta[...] = jnp.where(lane == 6, rounds.astype(F32), listed).astype(jnp.int32)


def plan(me, pairs, lengths, holder):
    devices = holder.shape[0]
    return pl.pallas_call(
        plan_kernel,
        out_shape=(
            jax.ShapeDtypeStruct((devices * FIRST // 2, 4 * devices), BF),
            jax.ShapeDtypeStruct((FIRST, 128), jnp.int32),
            jax.ShapeDtypeStruct((8, 2 * pairs.shape[0]), jnp.int32),
        ),
        in_specs=[SMEM] + [VMEM] * 3,
        out_specs=(VMEM,) * 3,
        compiler_params=pltpu.CompilerParams(vmem_limit_bytes=16 * MIB),
        cost_estimate=pl.CostEstimate(flops=10**9, bytes_accessed=10**6, transcendentals=0),
    )(me.reshape(1), pairs, lengths.reshape(1, -1), holder.reshape(1, -1))


def pick_kernel(selector_at, mine_at, picked_at, selector, mine, picked, units, sems):
    rows, _, half = mine.shape
    pieces = 2
    tall, deep = selector.shape[0] // pieces, picked.shape[0] // pieces
    arrive = [pltpu.make_async_copy(mine_at, mine, sems.at[2 * pieces])]
    leave = []
    for i in range(pieces):
        at, to = pl.ds(i * tall, tall), pl.ds(i * deep, deep)
        arrive.append(pltpu.make_async_copy(selector_at.at[at], selector.at[at], sems.at[i]))
        leave.append(pltpu.make_async_copy(picked.at[to], picked_at.at[to], sems.at[pieces + i]))
    for copy in arrive:
        copy.start()
    arrive[0].wait()
    units[:, :half] = mine[...].reshape(2 * rows, half)
    units[:, half:] = jnp.ones((2 * rows, 128), BF)
    low = iota((tall, 128), 1) < 64
    for i in range(pieces):
        arrive[1 + i].wait()
        at, to = slice(i * tall, (i + 1) * tall), slice(i * deep, (i + 1) * deep)
        tiles, rests = [], []
        for side in range(2):
            row = mm(selector[at, side * 2 * rows : (side + 1) * 2 * rows], units[...])
            left = row[:, half:] > 0.0
            for tile in range(2):
                one, two = tile * 128, 256 + tile * 128
                tiles.append(jnp.where(left, row[:, one : one + 128], -row[:, two : two + 128]))
            ends = row[:, 512:640]
            turned = half_turn(ends)
            rests.append(jnp.where(left, turned, -ends) if side else jnp.where(left, ends, -turned))
        tiles.append(jnp.where(low, rests[0], rests[1]))
        message = jnp.concatenate(tiles, axis=1).astype(BF)
        picked[to] = message.reshape((deep,) + picked.shape[1:])
        leave[i].start()
    for copy in leave:
        copy.wait()


def pick(selector, mine, outer):
    devices, _, half = mine.shape
    shape = (devices,) + outer + (half,)
    return pl.pallas_call(
        pick_kernel,
        out_shape=jax.ShapeDtypeStruct(shape, BF),
        in_specs=[ANY] * 2,
        out_specs=ANY,
        scratch_shapes=[
            pltpu.VMEM(selector.shape, BF),
            pltpu.VMEM(mine.shape, BF),
            pltpu.VMEM(shape, BF),
            pltpu.VMEM((2 * devices, half + 128), BF),
            pltpu.SemaphoreType.DMA((9,)),
        ],
        compiler_params=pltpu.CompilerParams(vmem_limit_bytes=16 * MIB),
        cost_estimate=pl.CostEstimate(flops=10**9, bytes_accessed=10**7, transcendentals=0),
    )(selector, mine)


def query_kernel(own, other, weight, query):
    first = iota((128, 128), 0) < HEAD_DIM
    for who, rows in enumerate((own, other)):
        result = mm(rows[...], weight[...]).astype(BF).astype(F32) * HEAD_DIM**-0.5
        width = result.shape[1]
        for pair in range(width // 128):
            at = slice(who * width + pair * 128, who * width + (pair + 1) * 128)
            tile = jnp.transpose(result[:, pair * 128 : (pair + 1) * 128])
            query[at, :128] = jnp.where(first, tile, 0.0).astype(BF)
            query[at, 128:] = jnp.where(first, 0.0, tile).astype(BF)


def queries(own, other, weight):
    return pl.pallas_call(
        query_kernel,
        out_shape=jax.ShapeDtypeStruct((2 * own.shape[1], 256), BF),
        in_specs=[VMEM] * 3,
        out_specs=VMEM,
        compiler_params=pltpu.CompilerParams(vmem_limit_bytes=12 * MIB),
        cost_estimate=pl.CostEstimate(flops=10**9, bytes_accessed=10**7, transcendentals=0),
    )(own, other, weight)


def attend_kernel(
    meta_at, got_at, query_at, k_at, v_at, o_at, own_at, out_at, sibling_at,
    meta, own, got, query, weight_k, weight_v, weight_o, rows, keys, values,
    context, scores, weights, scales, out, sibling, sems,
):
    def copy(index, source, target):
        return pltpu.make_async_copy(source, target, sems.at[index])

    quarters = []
    for quarter in range(4):
        at = pl.ds(quarter * BLOCK, BLOCK)
        quarters.append(copy(quarter, got_at.at[at], got.at[at]))
    copies = [
        copy(4 + i, a, b)
        for i, (a, b) in enumerate(
            [(meta_at, meta), (k_at, weight_k), (v_at, weight_v), (query_at, query), (o_at, weight_o),
             (own_at, own)]
        )
    ]
    for one in quarters + copies[:3]:
        one.start()
    width = weight_k.shape[0]
    each = 1
    for n in got.shape[1:-1]:
        each *= n
    tall = 16 * each
    context[...] = jnp.zeros_like(context)
    values[...] = jnp.zeros_like(values)
    lead, lane = iota((tall, tall), 0), iota((tall, tall), 1)
    n = jnp.int32(each)
    turned = (lead == lax.rem(lane, n) * 16 + lax.div(lane, n)).astype(BF)
    low = iota((tall, 128), 1) < 64
    rests = {}
    for quarter in range(4):
        quarters[quarter].wait()
        for part in range(2):
            at = quarter * BLOCK + part * 16
            piece = mm(turned, got[at : at + 16].reshape(tall, width // 2))
            rests[quarter, part] = piece[:, 512:640]
            piece = piece.astype(BF)
            for u in range(2 * each):
                to = u * BLOCK + part * 16
                side = (u % 2) * 256
                rows[to : to + 16, quarter * 256 : quarter * 256 + 256] = piece[
                    (u // 2) * 16 : (u // 2) * 16 + 16, side : side + 256
                ]
            if quarter % 2 == 1:
                left, right = rests[quarter - 1, part], rests[quarter, part]
                even = jnp.where(low, left, half_turn(right)).astype(BF)
                odd = jnp.where(low, half_turn(left), right).astype(BF)
                tile = 1024 + 128 * (quarter // 2)
                for u in range(2 * each):
                    to = u * BLOCK + part * 16
                    rows[to : to + 16, tile : tile + 128] = (odd if u % 2 else even)[
                        (u // 2) * 16 : (u // 2) * 16 + 16
                    ]
    copies[3].start()
    copies[4].start()
    copies[5].start()
    copies[0].wait()
    full = (meta[0, 7] + 3) // 8
    partial = (meta[0, 7] > full * 8).astype(jnp.int32)

    def project(weight, to):
        def some(first, size):
            at = pl.ds(pl.multiple_of(first, size), size)
            to[at, :] = mm(rows[at, :], weight[...]).astype(BF)

        def whole(chunk, carry):
            some(chunk * 256, 256)
            return carry

        def rest(chunk, carry):
            some(full * 256, 128)
            return carry

        lax.fori_loop(0, full, whole, 0)
        lax.fori_loop(0, partial, rest, 0)

    copies[1].wait()
    project(weight_k, keys)
    copies[2].wait()
    project(weight_v, values)
    copies[3].wait()

    def two_sides(index, carry):
        sides = [2 * index, 2 * index + 1]
        starts = [pl.multiple_of(meta[i, 0] * BLOCK, BLOCK) for i in sides]
        lengths = [meta[i, 1] for i in sides]
        whose = [meta[i, 2] for i in sides]
        pairs = range(width // 128)

        def with_keys(*sizes):
            positions = [iota((size, 256), 0) for size in sizes]

            def score(side, pair):
                at = slice(pair * 128, (pair + 1) * 128)
                first = pl.multiple_of(whose[side] * width + pair * 128, 128)
                size = sizes[side]
                result = mm(keys[pl.ds(starts[side], size), at], query[pl.ds(first, 128), :])
                scores[side, :size, pair * 256 : (pair + 1) * 256] = result

            def soften(side, pair):
                at = slice(pair * 256, (pair + 1) * 256)
                size = sizes[side]
                live = positions[side] < lengths[side]
                score = jnp.where(live, scores[side, :size, at], -1e30)
                power = jnp.exp(score - jnp.max(score, axis=0, keepdims=True))
                weights[side, :size, at] = power.astype(BF)
                scale = 1.0 / jnp.sum(power, axis=0, keepdims=True)
                scales[side, 0:1, at] = jnp.where(lengths[side] > 0, scale, 0.0)

            def gather(side, pair):
                at = slice(pair * 256, (pair + 1) * 256)
                size = sizes[side]
                v = values[pl.ds(starts[side], size), pair * 128 : (pair + 1) * 128]
                w = weights[side, :size, at]
                result = lax.dot_general(v, w, DOWN, preferred_element_type=F32)
                scale = scales[side, 0:1, at]
                to = pl.multiple_of(whose[side] * width + pair * 128, 128)
                context[pl.ds(to, 64), :] += result[:64, :128] * scale[:, :128]
                context[pl.ds(to + 64, 64), :] += result[64:, 128:] * scale[:, 128:]

            for pair in pairs:
                score(0, pair)
            for pair in pairs:
                score(1, pair)
                soften(0, pair)
            for pair in pairs:
                soften(1, pair)
                gather(0, pair)
            for pair in pairs:
                gather(1, pair)

        longer = [length > 64 for length in lengths]

        @pl.when(longer[1])
        def _():
            with_keys(128, 128)

        @pl.when(jnp.logical_and(longer[0], jnp.logical_not(longer[1])))
        def _():
            with_keys(128, 64)

        @pl.when(jnp.logical_not(jnp.logical_or(longer[0], longer[1])))
        def _():
            with_keys(64, 64)

        return carry

    lax.fori_loop(0, (meta[0, 3] + 1) // 2, two_sides, 0)
    copies[4].wait()
    copies[5].wait()
    part = context[width:, :].astype(BF)
    update = lax.dot_general(part, weight_o[...], DOWN, preferred_element_type=F32)
    sibling[...] = jnp.where(iota(update.shape, 0) < meta[0, 5], update, 0.0).astype(BF)
    leave = [copy(10, sibling, sibling_at)]
    leave[0].start()
    part = context[:width, :].astype(BF)
    for half in range(2):
        at = pl.ds(half * (width // 2), width // 2)
        update = lax.dot_general(part, weight_o[:, at], DOWN, preferred_element_type=F32)
        update = jnp.where(iota(update.shape, 0) < meta[0, 4], update, 0.0)
        out[:, at] = own[:, at].astype(F32) + update
        leave.append(copy(11 + half, out.at[:, at], out_at.at[:, at]))
        leave[-1].start()
    for one in leave:
        one.wait()


def attend(meta, got, query, weight_k, weight_v, weight_o, own):
    width = weight_k.shape[0]
    each = 1
    for n in got.shape[1:-1]:
        each *= n
    tall = 2 * each * BLOCK
    return pl.pallas_call(
        attend_kernel,
        out_shape=(
            jax.ShapeDtypeStruct((128, width), F32),
            jax.ShapeDtypeStruct((128, width), BF),
        ),
        in_specs=[ANY] * 7,
        out_specs=(ANY, ANY),
        scratch_shapes=[
            pltpu.SMEM(meta.shape, jnp.int32),
            pltpu.VMEM(own.shape, BF),
            pltpu.VMEM(got.shape, BF),
            pltpu.VMEM(query.shape, BF),
            pltpu.VMEM((width, width), BF),
            pltpu.VMEM((width, width), BF),
            pltpu.VMEM((width, width), BF),
            pltpu.VMEM((tall, width), BF),
            pltpu.VMEM((tall + (PARTS - 1) * BLOCK, width), BF),
            pltpu.VMEM((tall + (PARTS - 1) * BLOCK, width), BF),
            pltpu.VMEM((2 * width, 128), F32),
            pltpu.VMEM((2, 128, 2 * width), F32),
            pltpu.VMEM((2, 128, 2 * width), BF),
            pltpu.VMEM((2, 8, 2 * width), F32),
            pltpu.VMEM((128, width), F32),
            pltpu.VMEM((128, width), BF),
            pltpu.SemaphoreType.DMA((13,)),
        ],
        compiler_params=pltpu.CompilerParams(vmem_limit_bytes=36 * MIB),
        cost_estimate=pl.CostEstimate(flops=10**10, bytes_accessed=10**7, transcendentals=10**6),
    )(meta, got, query, weight_k, weight_v, weight_o, own)


def later_round(number, sides, me, count, meta):
    dest, source, length, amount, base, _, place, _ = sides
    origin = FIRST - PARTS + 1
    turn = jnp.where(base + amount <= FIRST, 0, 1 + (base - origin) // STEP)
    active = turn == number
    base = base - origin - (number - 1) * STEP
    spots = jnp.arange(LATER, dtype=jnp.int32)
    target = (dest[None, :] == jnp.arange(count, dtype=jnp.int32)[:, None]) & active[None, :]
    there = (base[:, None] <= spots) & (spots < (base + amount)[:, None])
    entries = [jnp.where(there, source[:, None] + 1, 0), jnp.where(there, spots - base[:, None], 0)]
    high, low = (mm(target.astype(BF), entry.astype(BF)).astype(jnp.int32) for entry in entries)
    unit = (4 * (high - 1) + low).reshape(-1, 2)
    columns = jnp.arange(2 * count, dtype=jnp.int32)
    selector = jnp.where((unit // 2)[:, :, None] == columns, (1 - 2 * (unit % 2))[:, :, None], 0)
    selector = selector.reshape(unit.shape[0], -1).astype(BF)
    held = active & (dest == me)
    order = jnp.sum(held[:, None] & (base[:, None] < base[None, :]), axis=0)
    chosen = held[None, :] & (order[None, :] == spots[:, None])

    def listed(values):
        return jnp.sum(jnp.where(chosen, values[None, :], 0), axis=1)

    held_count = jnp.broadcast_to(jnp.sum(held.astype(jnp.int32)), (LATER,))
    columns = [listed(base), listed(length), listed((place + me) % 2), held_count]
    meta = meta[:LATER].at[:, :4].set(jnp.stack(columns, axis=1))
    return selector, meta.at[:, 7].set(jnp.max(jnp.where(held, base + amount, 0)))


def local(embeddings, weight_q, weight_k, weight_v, weight_o, pairs, lengths, holder):
    count = lax.axis_size("group") * lax.axis_size("dev")
    me = lax.axis_index("group") * lax.axis_size("dev") + lax.axis_index("dev")
    own = embeddings[0]
    mine = exchange(front(own))
    selector, meta, sides = plan(me, pairs, lengths, holder)
    rounds = meta[0, 6]
    query = queries(own, swap(own), weight_q)

    def one_round(selector, meta, outer, base):
        got = exchange(pick(selector, mine, outer))
        return attend(meta, got, query, weight_k, weight_v, weight_o, base)

    def another(carry):
        number, total = carry
        nothing = jnp.zeros_like(own)
        kept, given = one_round(*later_round(number, sides, me, count, meta), (LATER // 2,), nothing)
        return number + 1, total + kept + swap(given).astype(F32)

    kept, given = one_round(selector, meta, (FIRST // 8, 4), own)
    received = swap(given)
    _, kept = lax.while_loop(lambda c: c[0] <= rounds, another, (jnp.int32(1), kept))
    return (kept + received.astype(F32)).astype(BF)[None]


def solution(mesh):
    in_specs = (P(AXES, None, None), P(), P(), P(), P(), P(), P(), P())
    out_specs = P(AXES, None, None)
    return jax.shard_map(local, mesh=mesh, in_specs=in_specs, out_specs=out_specs, check_vma=False)
```

```python
import jax
import jax.numpy as jnp
from jax import lax
from jax.experimental import pallas as pl
from jax.experimental.pallas import tpu as pltpu
from jax.sharding import PartitionSpec as P

HEAD_DIM = 64
AXES = ("group", "dev")
BLOCK = 32
PARTS = 4
FIRST = 24
LATER = 16
STEP = LATER - PARTS + 1
MIB = 1024 * 1024
BF = jnp.bfloat16
F32 = jnp.float32
VMEM = pl.BlockSpec(memory_space=pltpu.VMEM)
SMEM = pl.BlockSpec(memory_space=pltpu.SMEM)
HBM = pl.BlockSpec(memory_space=pltpu.HBM)
ACROSS = (((1,), (1,)), ((), ()))
DOWN = (((0,), (0,)), ((), ()))


def exchange(array):
    return lax.all_to_all(array, AXES, split_axis=0, concat_axis=0, tiled=True)


def swap(array):
    count = lax.axis_size("dev")
    return lax.ppermute(array, "dev", [(i, i ^ 1) for i in range(count)])


def mm(a, b):
    return jnp.dot(a, b, preferred_element_type=F32)


def iota(shape, dim):
    return lax.broadcasted_iota(jnp.int32, shape, dim)


def half_turn(array):
    return pltpu.roll(array.astype(F32), 64, 1)


def front_kernel(own_at, pieces_at, own, pieces, sems):
    low = iota((BLOCK, 128), 1) < 64
    arrive, leave = [], []
    for i in range(4):
        at = pl.ds(i * BLOCK, BLOCK)
        arrive.append(pltpu.make_async_copy(own_at.at[at], own.at[at], sems.at[i]))
        leave.append(pltpu.make_async_copy(pieces.at[at], pieces_at.at[at], sems.at[4 + i]))
    for copy in arrive:
        copy.start()
    for h in range(2):
        arrive[2 * h].wait()
        arrive[2 * h + 1].wait()
        even = slice(2 * h * BLOCK, (2 * h + 1) * BLOCK)
        odd = slice((2 * h + 1) * BLOCK, (2 * h + 2) * BLOCK)
        for quarter in range(4):
            main = slice(256 * quarter, 256 * quarter + 256)
            tile = slice(1024 + 128 * (quarter // 2), 1152 + 128 * (quarter // 2))
            if quarter % 2 == 0:
                rest = jnp.where(low, own[even, tile].astype(F32), half_turn(own[odd, tile]))
            else:
                rest = jnp.where(low, half_turn(own[even, tile]), own[odd, tile].astype(F32))
            to = slice(quarter * BLOCK, (quarter + 1) * BLOCK)
            pieces[to, h, 0:256] = own[even, main]
            pieces[to, h, 256:512] = own[odd, main]
            pieces[to, h, 512:640] = rest.astype(BF)
            if h == 1:
                leave[quarter].start()
    for copy in leave:
        copy.wait()


def front(own):
    rows, width = own.shape
    return pl.pallas_call(
        front_kernel,
        out_shape=jax.ShapeDtypeStruct((rows, 2, width // 2), BF),
        in_specs=[HBM],
        out_specs=HBM,
        scratch_shapes=[
            pltpu.VMEM((rows, width), BF),
            pltpu.VMEM((rows, 2, width // 2), BF),
            pltpu.SemaphoreType.DMA((8,)),
        ],
        compiler_params=pltpu.CompilerParams(vmem_limit_bytes=60 * MIB),
    )(own)


def plan_kernel(place, pairs, lengths, holder, selector, meta, sides):
    me = place[0]
    count = pairs.shape[0]
    total = 2 * count
    devices = holder.shape[1]
    lane = iota((count, devices), 1)
    marks = [pairs[:, i : i + 1] == lane for i in range(2)]
    held_at = holder[...].astype(F32)
    long = lengths[...].astype(F32)
    places = [jnp.sum(jnp.where(m, held_at, 0.0), axis=1, keepdims=True) for m in marks]
    sizes = [jnp.sum(jnp.where(m, long, 0.0), axis=1, keepdims=True) for m in marks]
    place_col = jnp.concatenate(places, axis=0)
    source_col = jnp.concatenate(places[::-1], axis=0)
    length_col = jnp.concatenate(sizes[::-1], axis=0)
    lane = iota((total, devices), 1)
    listed = jnp.where(lane == 0, place_col, jnp.where(lane == 1, source_col, length_col))
    turned = jnp.transpose(listed).astype(jnp.int32)
    place_row, source, length = turned[0:1], turned[1:2], turned[2:3]
    amount = (length + (BLOCK - 1)) // BLOCK
    amount_col = ((length_col.astype(jnp.int32) + (BLOCK - 1)) // BLOCK).astype(F32)
    chip = place_row // 2
    tied = (amount_col == amount.astype(F32)) & (iota((total, total), 0) < iota((total, total), 1))
    earlier = (amount_col > amount.astype(F32)) | tied
    same = place_col.astype(jnp.int32) // 2 == chip
    before = jnp.sum(jnp.where(same & earlier, 1.0, 0.0), axis=0, keepdims=True).astype(jnp.int32)
    dest = 2 * chip + ((before + 1) // 2) % 2
    dest_col = jnp.transpose(jnp.broadcast_to(dest.astype(F32), (devices, total)))[:, 0:1]
    alike = (dest_col.astype(jnp.int32) == dest) & earlier
    base = jnp.sum(jnp.where(alike, amount_col, 0.0), axis=0, keepdims=True).astype(jnp.int32)
    slot = jnp.sum(jnp.where(alike, 1.0, 0.0), axis=0, keepdims=True).astype(jnp.int32)
    sides[...] = jnp.concatenate(
        [dest, source, length, amount, base, slot, place_row, place_row], axis=0
    )
    active = base + amount <= FIRST
    spot = iota((devices, total), 0)
    target = jnp.where((dest == spot) & active, 1.0, 0.0).astype(BF)
    there = (base <= spot) & (spot < base + amount)
    entry = jnp.where(there, source + 1, 0)
    shifted = spot - 64
    entry = entry + jnp.where((base <= shifted) & (shifted < base + amount), shifted - base, 0)
    table = lax.dot_general(target, entry.astype(F32).astype(BF), ACROSS, preferred_element_type=F32)
    rows = devices * FIRST // 2
    row, lane = iota((rows, devices), 0), iota((rows, devices), 1)
    which, v = lax.div(row, jnp.int32(FIRST // 2)), lax.rem(row, jnp.int32(FIRST // 2))
    spread = mm(jnp.where(which == lane, 1.0, 0.0).astype(BF), table.astype(BF))
    columns = iota((rows, 2 * devices), 1)
    for side in range(2):
        u = 2 * v + side
        value = jnp.where(lane == u, 4.0 * spread, jnp.where(lane == u + 64, spread, 0.0))
        unit = jnp.sum(value, axis=1, keepdims=True).astype(jnp.int32) - 4
        sign = (1 - 2 * (unit % 2)).astype(F32)
        at = slice(side * 2 * devices, (side + 1) * 2 * devices)
        selector[:, at] = jnp.where(unit // 2 == columns, sign, 0.0).astype(BF)
    held = active & (dest == me)
    chosen = held & (slot == iota((FIRST, total), 0))

    def column(values):
        return jnp.sum(jnp.where(chosen, values.astype(F32), 0.0), axis=1, keepdims=True)

    amount_held = jnp.sum(jnp.where(held, 1.0, 0.0), axis=1, keepdims=True)
    rounds = jnp.max(jnp.where(active, 0, 1 + (base - (FIRST - PARTS + 1)) // STEP), axis=1, keepdims=True)
    ends = [
        jnp.sum(jnp.where(holder[...] == which, long, 0.0), axis=1, keepdims=True)
        for which in (me, me + 1 - 2 * (me % 2))
    ]
    lane = iota(meta.shape, 1)
    listed = jnp.where(lane == 1, column(length), column(base))
    listed = jnp.where(lane == 2, column((place_row + me) % 2), listed)
    listed = jnp.where(lane == 3, amount_held, listed)
    blocks = jnp.max(jnp.where(held, base + amount, 0), axis=1, keepdims=True).astype(F32)
    listed = jnp.where(lane == 7, blocks, listed)
    listed = jnp.where(lane == 4, ends[0], jnp.where(lane == 5, ends[1], listed))
    meta[...] = jnp.where(lane == 6, rounds.astype(F32), listed).astype(jnp.int32)


def plan(me, pairs, lengths, holder):
    devices = holder.shape[0]
    return pl.pallas_call(
        plan_kernel,
        out_shape=(
            jax.ShapeDtypeStruct((devices * FIRST // 2, 4 * devices), BF),
            jax.ShapeDtypeStruct((FIRST, 128), jnp.int32),
            jax.ShapeDtypeStruct((8, 2 * pairs.shape[0]), jnp.int32),
        ),
        in_specs=[SMEM] + [VMEM] * 3,
        out_specs=(VMEM,) * 3,
        compiler_params=pltpu.CompilerParams(vmem_limit_bytes=16 * MIB),
        cost_estimate=pl.CostEstimate(flops=10**9, bytes_accessed=10**6, transcendentals=0),
    )(me.reshape(1), pairs, lengths.reshape(1, -1), holder.reshape(1, -1))


def pick_kernel(selector_at, mine_at, picked_at, selector, mine, picked, units, sems):
    rows, _, half = mine.shape
    pieces = 2
    tall, deep = selector.shape[0] // pieces, picked.shape[0] // pieces
    arrive = [pltpu.make_async_copy(mine_at, mine, sems.at[2 * pieces])]
    leave = []
    for i in range(pieces):
        at, to = pl.ds(i * tall, tall), pl.ds(i * deep, deep)
        arrive.append(pltpu.make_async_copy(selector_at.at[at], selector.at[at], sems.at[i]))
        leave.append(pltpu.make_async_copy(picked.at[to], picked_at.at[to], sems.at[pieces + i]))
    for copy in arrive:
        copy.start()
    arrive[0].wait()
    units[:, :half] = mine[...].reshape(2 * rows, half)
    units[:, half:] = jnp.ones((2 * rows, 128), BF)
    low = iota((tall, 128), 1) < 64
    for i in range(pieces):
        arrive[1 + i].wait()
        at, to = slice(i * tall, (i + 1) * tall), slice(i * deep, (i + 1) * deep)
        tiles, rests = [], []
        for side in range(2):
            row = mm(selector[at, side * 2 * rows : (side + 1) * 2 * rows], units[...])
            left = row[:, half:] > 0.0
            for tile in range(2):
                one, two = tile * 128, 256 + tile * 128
                tiles.append(jnp.where(left, row[:, one : one + 128], -row[:, two : two + 128]))
            ends = row[:, 512:640]
            turned = half_turn(ends)
            rests.append(jnp.where(left, turned, -ends) if side else jnp.where(left, ends, -turned))
        tiles.append(jnp.where(low, rests[0], rests[1]))
        message = jnp.concatenate(tiles, axis=1).astype(BF)
        picked[to] = message.reshape((deep,) + picked.shape[1:])
        leave[i].start()
    for copy in leave:
        copy.wait()


def pick(selector, mine, outer):
    devices, _, half = mine.shape
    shape = (devices,) + outer + (half,)
    return pl.pallas_call(
        pick_kernel,
        out_shape=jax.ShapeDtypeStruct(shape, BF),
        in_specs=[HBM] * 2,
        out_specs=HBM,
        scratch_shapes=[
            pltpu.VMEM(selector.shape, BF),
            pltpu.VMEM(mine.shape, BF),
            pltpu.VMEM(shape, BF),
            pltpu.VMEM((2 * devices, half + 128), BF),
            pltpu.SemaphoreType.DMA((9,)),
        ],
        compiler_params=pltpu.CompilerParams(vmem_limit_bytes=16 * MIB),
        cost_estimate=pl.CostEstimate(flops=10**9, bytes_accessed=10**7, transcendentals=0),
    )(selector, mine)


def query_kernel(own, other, weight, query):
    first = iota((128, 128), 0) < HEAD_DIM
    for who, rows in enumerate((own, other)):
        result = mm(rows[...], weight[...]).astype(BF).astype(F32) * HEAD_DIM**-0.5
        width = result.shape[1]
        for pair in range(width // 128):
            at = slice(who * width + pair * 128, who * width + (pair + 1) * 128)
            tile = jnp.transpose(result[:, pair * 128 : (pair + 1) * 128])
            query[at, :128] = jnp.where(first, tile, 0.0).astype(BF)
            query[at, 128:] = jnp.where(first, 0.0, tile).astype(BF)


def queries(own, other, weight):
    return pl.pallas_call(
        query_kernel,
        out_shape=jax.ShapeDtypeStruct((2 * own.shape[1], 256), BF),
        in_specs=[VMEM] * 3,
        out_specs=VMEM,
        compiler_params=pltpu.CompilerParams(vmem_limit_bytes=12 * MIB),
        cost_estimate=pl.CostEstimate(flops=10**9, bytes_accessed=10**7, transcendentals=0),
    )(own, other, weight)


def attend_kernel(
    meta_at, got_at, query_at, k_at, v_at, o_at, out_at, sibling_at,
    meta, got, query, weight_k, weight_v, weight_o, rows, keys, values,
    context, scores, weights, scales, out, sibling, sems,
):
    def copy(index, source, target):
        return pltpu.make_async_copy(source, target, sems.at[index])

    quarters = []
    for quarter in range(4):
        at = pl.ds(quarter * BLOCK, BLOCK)
        quarters.append(copy(quarter, got_at.at[at], got.at[at]))
    copies = [
        copy(4 + i, a, b)
        for i, (a, b) in enumerate(
            [(meta_at, meta), (k_at, weight_k), (v_at, weight_v), (query_at, query), (o_at, weight_o)]
        )
    ]
    for one in quarters + copies[:3]:
        one.start()
    width = weight_k.shape[0]
    each = 1
    for n in got.shape[1:-1]:
        each *= n
    tall = 16 * each
    context[...] = jnp.zeros_like(context)
    values[...] = jnp.zeros_like(values)
    lead, lane = iota((tall, tall), 0), iota((tall, tall), 1)
    n = jnp.int32(each)
    turned = (lead == lax.rem(lane, n) * 16 + lax.div(lane, n)).astype(BF)
    low = iota((tall, 128), 1) < 64
    rests = {}
    for quarter in range(4):
        quarters[quarter].wait()
        for part in range(2):
            at = quarter * BLOCK + part * 16
            piece = mm(turned, got[at : at + 16].reshape(tall, width // 2))
            rests[quarter, part] = piece[:, 512:640]
            piece = piece.astype(BF)
            for u in range(2 * each):
                to = u * BLOCK + part * 16
                side = (u % 2) * 256
                rows[to : to + 16, quarter * 256 : quarter * 256 + 256] = piece[
                    (u // 2) * 16 : (u // 2) * 16 + 16, side : side + 256
                ]
            if quarter % 2 == 1:
                left, right = rests[quarter - 1, part], rests[quarter, part]
                even = jnp.where(low, left, half_turn(right)).astype(BF)
                odd = jnp.where(low, half_turn(left), right).astype(BF)
                tile = 1024 + 128 * (quarter // 2)
                for u in range(2 * each):
                    to = u * BLOCK + part * 16
                    rows[to : to + 16, tile : tile + 128] = (odd if u % 2 else even)[
                        (u // 2) * 16 : (u // 2) * 16 + 16
                    ]
    copies[3].start()
    copies[4].start()
    copies[0].wait()
    full = (meta[0, 7] + 3) // 8
    partial = (meta[0, 7] > full * 8).astype(jnp.int32)

    def project(weight, to):
        def some(first, size):
            at = pl.ds(pl.multiple_of(first, size), size)
            to[at, :] = mm(rows[at, :], weight[...]).astype(BF)

        def whole(chunk, carry):
            some(chunk * 256, 256)
            return carry

        def rest(chunk, carry):
            some(full * 256, 128)
            return carry

        lax.fori_loop(0, full, whole, 0)
        lax.fori_loop(0, partial, rest, 0)

    copies[1].wait()
    project(weight_k, keys)
    copies[2].wait()
    project(weight_v, values)
    copies[3].wait()

    def two_sides(index, carry):
        sides = [2 * index, 2 * index + 1]
        starts = [pl.multiple_of(meta[i, 0] * BLOCK, BLOCK) for i in sides]
        lengths = [meta[i, 1] for i in sides]
        whose = [meta[i, 2] for i in sides]
        pairs = range(width // 128)

        def with_keys(*sizes):
            positions = [iota((size, 256), 0) for size in sizes]

            def score(side, pair):
                at = slice(pair * 128, (pair + 1) * 128)
                first = pl.multiple_of(whose[side] * width + pair * 128, 128)
                size = sizes[side]
                result = mm(keys[pl.ds(starts[side], size), at], query[pl.ds(first, 128), :])
                scores[side, :size, pair * 256 : (pair + 1) * 256] = result

            def soften(side, pair):
                at = slice(pair * 256, (pair + 1) * 256)
                size = sizes[side]
                live = positions[side] < lengths[side]
                score = jnp.where(live, scores[side, :size, at], -1e30)
                power = jnp.exp(score - jnp.max(score, axis=0, keepdims=True))
                weights[side, :size, at] = power.astype(BF)
                scale = 1.0 / jnp.sum(power, axis=0, keepdims=True)
                scales[side, 0:1, at] = jnp.where(lengths[side] > 0, scale, 0.0)

            def gather(side, pair):
                at = slice(pair * 256, (pair + 1) * 256)
                size = sizes[side]
                v = values[pl.ds(starts[side], size), pair * 128 : (pair + 1) * 128]
                w = weights[side, :size, at]
                result = lax.dot_general(v, w, DOWN, preferred_element_type=F32)
                scale = scales[side, 0:1, at]
                to = pl.multiple_of(whose[side] * width + pair * 128, 128)
                context[pl.ds(to, 64), :] += result[:64, :128] * scale[:, :128]
                context[pl.ds(to + 64, 64), :] += result[64:, 128:] * scale[:, 128:]

            for pair in pairs:
                score(0, pair)
            for pair in pairs:
                score(1, pair)
                soften(0, pair)
            for pair in pairs:
                soften(1, pair)
                gather(0, pair)
            for pair in pairs:
                gather(1, pair)

        longer = [length > 64 for length in lengths]

        @pl.when(longer[1])
        def _():
            with_keys(128, 128)

        @pl.when(jnp.logical_and(longer[0], jnp.logical_not(longer[1])))
        def _():
            with_keys(128, 64)

        @pl.when(jnp.logical_not(jnp.logical_or(longer[0], longer[1])))
        def _():
            with_keys(64, 64)

        return carry

    lax.fori_loop(0, (meta[0, 3] + 1) // 2, two_sides, 0)
    copies[4].wait()
    part = context[width:, :].astype(BF)
    update = lax.dot_general(part, weight_o[...], DOWN, preferred_element_type=F32)
    sibling[...] = jnp.where(iota(update.shape, 0) < meta[0, 5], update, 0.0).astype(BF)
    leave = [copy(9, sibling, sibling_at)]
    leave[0].start()
    part = context[:width, :].astype(BF)
    for half in range(2):
        at = pl.ds(half * (width // 2), width // 2)
        update = lax.dot_general(part, weight_o[:, at], DOWN, preferred_element_type=F32)
        out[:, at] = jnp.where(iota(update.shape, 0) < meta[0, 4], update, 0.0)
        leave.append(copy(10 + half, out.at[:, at], out_at.at[:, at]))
        leave[-1].start()
    for one in leave:
        one.wait()


def attend(meta, got, query, weight_k, weight_v, weight_o):
    width = weight_k.shape[0]
    each = 1
    for n in got.shape[1:-1]:
        each *= n
    tall = 2 * each * BLOCK
    return pl.pallas_call(
        attend_kernel,
        out_shape=(
            jax.ShapeDtypeStruct((128, width), F32),
            jax.ShapeDtypeStruct((128, width), BF),
        ),
        in_specs=[HBM] * 6,
        out_specs=(HBM, HBM),
        scratch_shapes=[
            pltpu.SMEM(meta.shape, jnp.int32),
            pltpu.VMEM(got.shape, BF),
            pltpu.VMEM(query.shape, BF),
            pltpu.VMEM((width, width), BF),
            pltpu.VMEM((width, width), BF),
            pltpu.VMEM((width, width), BF),
            pltpu.VMEM((tall, width), BF),
            pltpu.VMEM((tall + (PARTS - 1) * BLOCK, width), BF),
            pltpu.VMEM((tall + (PARTS - 1) * BLOCK, width), BF),
            pltpu.VMEM((2 * width, 128), F32),
            pltpu.VMEM((2, 128, 2 * width), F32),
            pltpu.VMEM((2, 128, 2 * width), BF),
            pltpu.VMEM((2, 8, 2 * width), F32),
            pltpu.VMEM((128, width), F32),
            pltpu.VMEM((128, width), BF),
            pltpu.SemaphoreType.DMA((12,)),
        ],
        compiler_params=pltpu.CompilerParams(vmem_limit_bytes=36 * MIB),
        cost_estimate=pl.CostEstimate(flops=10**10, bytes_accessed=10**7, transcendentals=10**6),
    )(meta, got, query, weight_k, weight_v, weight_o)


def later_round(number, sides, me, count, meta):
    dest, source, length, amount, base, _, place, _ = sides
    origin = FIRST - PARTS + 1
    turn = jnp.where(base + amount <= FIRST, 0, 1 + (base - origin) // STEP)
    active = turn == number
    base = base - origin - (number - 1) * STEP
    spots = jnp.arange(LATER, dtype=jnp.int32)
    target = (dest[None, :] == jnp.arange(count, dtype=jnp.int32)[:, None]) & active[None, :]
    there = (base[:, None] <= spots) & (spots < (base + amount)[:, None])
    entries = [jnp.where(there, source[:, None] + 1, 0), jnp.where(there, spots - base[:, None], 0)]
    high, low = (mm(target.astype(BF), entry.astype(BF)).astype(jnp.int32) for entry in entries)
    unit = (4 * (high - 1) + low).reshape(-1, 2)
    columns = jnp.arange(2 * count, dtype=jnp.int32)
    selector = jnp.where((unit // 2)[:, :, None] == columns, (1 - 2 * (unit % 2))[:, :, None], 0)
    selector = selector.reshape(unit.shape[0], -1).astype(BF)
    held = active & (dest == me)
    order = jnp.sum(held[:, None] & (base[:, None] < base[None, :]), axis=0)
    chosen = held[None, :] & (order[None, :] == spots[:, None])

    def listed(values):
        return jnp.sum(jnp.where(chosen, values[None, :], 0), axis=1)

    held_count = jnp.broadcast_to(jnp.sum(held.astype(jnp.int32)), (LATER,))
    columns = [listed(base), listed(length), listed((place + me) % 2), held_count]
    meta = meta[:LATER].at[:, :4].set(jnp.stack(columns, axis=1))
    return selector, meta.at[:, 7].set(jnp.max(jnp.where(held, base + amount, 0)))


def local(embeddings, weight_q, weight_k, weight_v, weight_o, pairs, lengths, holder):
    count = lax.axis_size("group") * lax.axis_size("dev")
    me = lax.axis_index("group") * lax.axis_size("dev") + lax.axis_index("dev")
    own = embeddings[0]
    mine = exchange(front(own))
    selector, meta, sides = plan(me, pairs, lengths, holder)
    rounds = meta[0, 6]
    query = queries(own, swap(own), weight_q)

    def one_round(selector, meta, outer):
        got = exchange(pick(selector, mine, outer))
        return attend(meta, got, query, weight_k, weight_v, weight_o)

    def another(carry):
        number, total = carry
        kept, given = one_round(*later_round(number, sides, me, count, meta), (LATER // 2,))
        return number + 1, total + kept + swap(given).astype(F32)

    kept, given = one_round(selector, meta, (FIRST // 8, 4))
    received = swap(given)
    _, kept = lax.while_loop(lambda c: c[0] <= rounds, another, (jnp.int32(1), kept))
    return (own.astype(F32) + (kept + received.astype(F32))).astype(BF)[None]


def solution(mesh):
    in_specs = (P(AXES, None, None), P(), P(), P(), P(), P(), P(), P())
    out_specs = P(AXES, None, None)
    return jax.shard_map(local, mesh=mesh, in_specs=in_specs, out_specs=out_specs, check_vma=False)
```

```python
import jax
import jax.numpy as jnp
from jax import lax
from jax.experimental import pallas as pl
from jax.experimental.pallas import tpu as pltpu
from jax.sharding import PartitionSpec as P

HEAD_DIM = 64
AXES = ("group", "dev")
BLOCK = 32
PARTS = 4
FIRST = 24
LATER = 16
STEP = LATER - PARTS + 1
MIB = 1024 * 1024
BF = jnp.bfloat16
F32 = jnp.float32
VMEM = pl.BlockSpec(memory_space=pltpu.VMEM)
SMEM = pl.BlockSpec(memory_space=pltpu.SMEM)
HBM = pl.BlockSpec(memory_space=pltpu.HBM)
ACROSS = (((1,), (1,)), ((), ()))
DOWN = (((0,), (0,)), ((), ()))


def exchange(array):
    return lax.all_to_all(array, AXES, split_axis=0, concat_axis=0, tiled=True)


def swap(array):
    count = lax.axis_size("dev")
    return lax.ppermute(array, "dev", [(i, i ^ 1) for i in range(count)])


def mm(a, b):
    return jnp.dot(a, b, preferred_element_type=F32)


def iota(shape, dim):
    return lax.broadcasted_iota(jnp.int32, shape, dim)


def half_turn(array):
    return pltpu.roll(array.astype(F32), 64, 1)


def front_kernel(own_at, pieces_at, own, pieces, sems):
    low = iota((BLOCK, 128), 1) < 64
    arrive, leave = [], []
    for i in range(4):
        at = pl.ds(i * BLOCK, BLOCK)
        arrive.append(pltpu.make_async_copy(own_at.at[at], own.at[at], sems.at[i]))
        leave.append(pltpu.make_async_copy(pieces.at[at], pieces_at.at[at], sems.at[4 + i]))
    for copy in arrive:
        copy.start()
    for h in range(2):
        arrive[2 * h].wait()
        arrive[2 * h + 1].wait()
        even = slice(2 * h * BLOCK, (2 * h + 1) * BLOCK)
        odd = slice((2 * h + 1) * BLOCK, (2 * h + 2) * BLOCK)
        for quarter in range(4):
            main = slice(256 * quarter, 256 * quarter + 256)
            tile = slice(1024 + 128 * (quarter // 2), 1152 + 128 * (quarter // 2))
            if quarter % 2 == 0:
                rest = jnp.where(low, own[even, tile].astype(F32), half_turn(own[odd, tile]))
            else:
                rest = jnp.where(low, half_turn(own[even, tile]), own[odd, tile].astype(F32))
            to = slice(quarter * BLOCK, (quarter + 1) * BLOCK)
            pieces[to, h, 0:256] = own[even, main]
            pieces[to, h, 256:512] = own[odd, main]
            pieces[to, h, 512:640] = rest.astype(BF)
            if h == 1:
                leave[quarter].start()
    for copy in leave:
        copy.wait()


def front(own):
    rows, width = own.shape
    return pl.pallas_call(
        front_kernel,
        out_shape=jax.ShapeDtypeStruct((rows, 2, width // 2), BF),
        in_specs=[HBM],
        out_specs=HBM,
        scratch_shapes=[
            pltpu.VMEM((rows, width), BF),
            pltpu.VMEM((rows, 2, width // 2), BF),
            pltpu.SemaphoreType.DMA((8,)),
        ],
        compiler_params=pltpu.CompilerParams(vmem_limit_bytes=60 * MIB),
    )(own)


def plan_kernel(place, pairs, lengths, holder, selector, meta, sides):
    me = place[0]
    count = pairs.shape[0]
    total = 2 * count
    devices = holder.shape[1]
    lane = iota((count, devices), 1)
    marks = [pairs[:, i : i + 1] == lane for i in range(2)]
    held_at = holder[...].astype(F32)
    long = lengths[...].astype(F32)
    places = [jnp.sum(jnp.where(m, held_at, 0.0), axis=1, keepdims=True) for m in marks]
    sizes = [jnp.sum(jnp.where(m, long, 0.0), axis=1, keepdims=True) for m in marks]
    place_col = jnp.concatenate(places, axis=0)
    source_col = jnp.concatenate(places[::-1], axis=0)
    length_col = jnp.concatenate(sizes[::-1], axis=0)
    lane = iota((total, devices), 1)
    listed = jnp.where(lane == 0, place_col, jnp.where(lane == 1, source_col, length_col))
    turned = jnp.transpose(listed).astype(jnp.int32)
    place_row, source, length = turned[0:1], turned[1:2], turned[2:3]
    amount = (length + (BLOCK - 1)) // BLOCK
    amount_col = ((length_col.astype(jnp.int32) + (BLOCK - 1)) // BLOCK).astype(F32)
    chip = place_row // 2
    tied = (amount_col == amount.astype(F32)) & (iota((total, total), 0) < iota((total, total), 1))
    earlier = (amount_col > amount.astype(F32)) | tied
    same = place_col.astype(jnp.int32) // 2 == chip
    before = jnp.sum(jnp.where(same & earlier, 1.0, 0.0), axis=0, keepdims=True).astype(jnp.int32)
    dest = 2 * chip + ((before + 1) // 2) % 2
    dest_col = jnp.transpose(jnp.broadcast_to(dest.astype(F32), (devices, total)))[:, 0:1]
    alike = (dest_col.astype(jnp.int32) == dest) & earlier
    base = jnp.sum(jnp.where(alike, amount_col, 0.0), axis=0, keepdims=True).astype(jnp.int32)
    slot = jnp.sum(jnp.where(alike, 1.0, 0.0), axis=0, keepdims=True).astype(jnp.int32)
    sides[...] = jnp.concatenate(
        [dest, source, length, amount, base, slot, place_row, place_row], axis=0
    )
    active = base + amount <= FIRST
    spot = iota((devices, total), 0)
    target = jnp.where((dest == spot) & active, 1.0, 0.0).astype(BF)
    there = (base <= spot) & (spot < base + amount)
    entry = jnp.where(there, source + 1, 0)
    shifted = spot - 64
    entry = entry + jnp.where((base <= shifted) & (shifted < base + amount), shifted - base, 0)
    table = lax.dot_general(target, entry.astype(F32).astype(BF), ACROSS, preferred_element_type=F32)
    rows = devices * FIRST // 2
    row, lane = iota((rows, devices), 0), iota((rows, devices), 1)
    which, v = lax.div(row, jnp.int32(FIRST // 2)), lax.rem(row, jnp.int32(FIRST // 2))
    spread = mm(jnp.where(which == lane, 1.0, 0.0).astype(BF), table.astype(BF))
    columns = iota((rows, 2 * devices), 1)
    for side in range(2):
        u = 2 * v + side
        value = jnp.where(lane == u, 4.0 * spread, jnp.where(lane == u + 64, spread, 0.0))
        unit = jnp.sum(value, axis=1, keepdims=True).astype(jnp.int32) - 4
        sign = (1 - 2 * (unit % 2)).astype(F32)
        at = slice(side * 2 * devices, (side + 1) * 2 * devices)
        selector[:, at] = jnp.where(unit // 2 == columns, sign, 0.0).astype(BF)
    held = active & (dest == me)
    chosen = held & (slot == iota((FIRST, total), 0))

    def column(values):
        return jnp.sum(jnp.where(chosen, values.astype(F32), 0.0), axis=1, keepdims=True)

    amount_held = jnp.sum(jnp.where(held, 1.0, 0.0), axis=1, keepdims=True)
    rounds = jnp.max(jnp.where(active, 0, 1 + (base - (FIRST - PARTS + 1)) // STEP), axis=1, keepdims=True)
    ends = [
        jnp.sum(jnp.where(holder[...] == which, long, 0.0), axis=1, keepdims=True)
        for which in (me, me + 1 - 2 * (me % 2))
    ]
    lane = iota(meta.shape, 1)
    listed = jnp.where(lane == 1, column(length), column(base))
    listed = jnp.where(lane == 2, column((place_row + me) % 2), listed)
    listed = jnp.where(lane == 3, amount_held, listed)
    blocks = jnp.max(jnp.where(held, base + amount, 0), axis=1, keepdims=True).astype(F32)
    listed = jnp.where(lane == 7, blocks, listed)
    listed = jnp.where(lane == 4, ends[0], jnp.where(lane == 5, ends[1], listed))
    meta[...] = jnp.where(lane == 6, rounds.astype(F32), listed).astype(jnp.int32)


def plan(me, pairs, lengths, holder):
    devices = holder.shape[0]
    return pl.pallas_call(
        plan_kernel,
        out_shape=(
            jax.ShapeDtypeStruct((devices * FIRST // 2, 4 * devices), BF),
            jax.ShapeDtypeStruct((FIRST, 128), jnp.int32),
            jax.ShapeDtypeStruct((8, 2 * pairs.shape[0]), jnp.int32),
        ),
        in_specs=[SMEM] + [VMEM] * 3,
        out_specs=(VMEM,) * 3,
        compiler_params=pltpu.CompilerParams(vmem_limit_bytes=16 * MIB),
        cost_estimate=pl.CostEstimate(flops=10**9, bytes_accessed=10**6, transcendentals=0),
    )(me.reshape(1), pairs, lengths.reshape(1, -1), holder.reshape(1, -1))


def pick_kernel(selector_at, mine_at, picked_at, selector, mine, picked, units, sems):
    rows, _, half = mine.shape
    pieces = 2
    tall, deep = selector.shape[0] // pieces, picked.shape[0] // pieces
    arrive = [pltpu.make_async_copy(mine_at, mine, sems.at[2 * pieces])]
    leave = []
    for i in range(pieces):
        at, to = pl.ds(i * tall, tall), pl.ds(i * deep, deep)
        arrive.append(pltpu.make_async_copy(selector_at.at[at], selector.at[at], sems.at[i]))
        leave.append(pltpu.make_async_copy(picked.at[to], picked_at.at[to], sems.at[pieces + i]))
    for copy in arrive:
        copy.start()
    arrive[0].wait()
    units[:, :half] = mine[...].reshape(2 * rows, half)
    units[:, half:] = jnp.ones((2 * rows, 128), BF)
    low = iota((tall, 128), 1) < 64
    for i in range(pieces):
        arrive[1 + i].wait()
        at, to = slice(i * tall, (i + 1) * tall), slice(i * deep, (i + 1) * deep)
        tiles, rests = [], []
        for side in range(2):
            row = mm(selector[at, side * 2 * rows : (side + 1) * 2 * rows], units[...])
            left = row[:, half:] > 0.0
            for tile in range(2):
                one, two = tile * 128, 256 + tile * 128
                tiles.append(jnp.where(left, row[:, one : one + 128], -row[:, two : two + 128]))
            ends = row[:, 512:640]
            turned = half_turn(ends)
            rests.append(jnp.where(left, turned, -ends) if side else jnp.where(left, ends, -turned))
        tiles.append(jnp.where(low, rests[0], rests[1]))
        message = jnp.concatenate(tiles, axis=1).astype(BF)
        picked[to] = message.reshape((deep,) + picked.shape[1:])
        leave[i].start()
    for copy in leave:
        copy.wait()


def pick(selector, mine, outer):
    devices, _, half = mine.shape
    shape = (devices,) + outer + (half,)
    return pl.pallas_call(
        pick_kernel,
        out_shape=jax.ShapeDtypeStruct(shape, BF),
        in_specs=[HBM] * 2,
        out_specs=HBM,
        scratch_shapes=[
            pltpu.VMEM(selector.shape, BF),
            pltpu.VMEM(mine.shape, BF),
            pltpu.VMEM(shape, BF),
            pltpu.VMEM((2 * devices, half + 128), BF),
            pltpu.SemaphoreType.DMA((9,)),
        ],
        compiler_params=pltpu.CompilerParams(vmem_limit_bytes=16 * MIB),
        cost_estimate=pl.CostEstimate(flops=10**9, bytes_accessed=10**7, transcendentals=0),
    )(selector, mine)


def query_kernel(own, other, weight, query):
    first = iota((128, 128), 0) < HEAD_DIM
    for who, rows in enumerate((own, other)):
        result = mm(rows[...], weight[...]).astype(BF).astype(F32) * HEAD_DIM**-0.5
        width = result.shape[1]
        for pair in range(width // 128):
            at = slice(who * width + pair * 128, who * width + (pair + 1) * 128)
            tile = jnp.transpose(result[:, pair * 128 : (pair + 1) * 128])
            query[at, :128] = jnp.where(first, tile, 0.0).astype(BF)
            query[at, 128:] = jnp.where(first, 0.0, tile).astype(BF)


def queries(own, other, weight):
    return pl.pallas_call(
        query_kernel,
        out_shape=jax.ShapeDtypeStruct((2 * own.shape[1], 256), BF),
        in_specs=[VMEM] * 3,
        out_specs=VMEM,
        compiler_params=pltpu.CompilerParams(vmem_limit_bytes=12 * MIB),
        cost_estimate=pl.CostEstimate(flops=10**9, bytes_accessed=10**7, transcendentals=0),
    )(own, other, weight)


def attend_kernel(
    meta_at, got_at, query_at, k_at, v_at, o_at, out_at, sibling_at,
    meta, got, query, weight_k, weight_v, weight_o, rows, keys, values,
    context, scores, weights, scales, out, sibling, sems,
):
    def copy(index, source, target):
        return pltpu.make_async_copy(source, target, sems.at[index])

    quarters = []
    for quarter in range(4):
        at = pl.ds(quarter * BLOCK, BLOCK)
        quarters.append(copy(quarter, got_at.at[at], got.at[at]))
    copies = [
        copy(4 + i, a, b)
        for i, (a, b) in enumerate(
            [(meta_at, meta), (k_at, weight_k), (v_at, weight_v), (query_at, query), (o_at, weight_o)]
        )
    ]
    for one in quarters + copies[:3]:
        one.start()
    width = weight_k.shape[0]
    each = 1
    for n in got.shape[1:-1]:
        each *= n
    tall = 16 * each
    context[...] = jnp.zeros_like(context)
    values[...] = jnp.zeros_like(values)
    lead, lane = iota((tall, tall), 0), iota((tall, tall), 1)
    n = jnp.int32(each)
    turned = (lead == lax.rem(lane, n) * 16 + lax.div(lane, n)).astype(BF)
    low = iota((tall, 128), 1) < 64
    rests = {}
    for quarter in range(4):
        quarters[quarter].wait()
        for part in range(2):
            at = quarter * BLOCK + part * 16
            piece = mm(turned, got[at : at + 16].reshape(tall, width // 2))
            rests[quarter, part] = piece[:, 512:640]
            piece = piece.astype(BF)
            for u in range(2 * each):
                to = u * BLOCK + part * 16
                side = (u % 2) * 256
                rows[to : to + 16, quarter * 256 : quarter * 256 + 256] = piece[
                    (u // 2) * 16 : (u // 2) * 16 + 16, side : side + 256
                ]
            if quarter % 2 == 1:
                left, right = rests[quarter - 1, part], rests[quarter, part]
                even = jnp.where(low, left, half_turn(right)).astype(BF)
                odd = jnp.where(low, half_turn(left), right).astype(BF)
                tile = 1024 + 128 * (quarter // 2)
                for u in range(2 * each):
                    to = u * BLOCK + part * 16
                    rows[to : to + 16, tile : tile + 128] = (odd if u % 2 else even)[
                        (u // 2) * 16 : (u // 2) * 16 + 16
                    ]
    copies[3].start()
    copies[4].start()
    copies[0].wait()
    full = (meta[0, 7] + 3) // 8
    partial = (meta[0, 7] > full * 8).astype(jnp.int32)

    def project(weight, to):
        def some(first, size):
            at = pl.ds(pl.multiple_of(first, size), size)
            to[at, :] = mm(rows[at, :], weight[...]).astype(BF)

        def whole(chunk, carry):
            some(chunk * 256, 256)
            return carry

        def rest(chunk, carry):
            some(full * 256, 128)
            return carry

        lax.fori_loop(0, full, whole, 0)
        lax.fori_loop(0, partial, rest, 0)

    copies[1].wait()
    project(weight_k, keys)
    copies[2].wait()
    project(weight_v, values)
    copies[3].wait()

    def two_sides(index, carry):
        sides = [2 * index, 2 * index + 1]
        starts = [pl.multiple_of(meta[i, 0] * BLOCK, BLOCK) for i in sides]
        lengths = [meta[i, 1] for i in sides]
        whose = [meta[i, 2] for i in sides]
        pairs = range(width // 128)

        def with_keys(*sizes):
            positions = [iota((size, 256), 0) for size in sizes]

            def score(side, pair):
                at = slice(pair * 128, (pair + 1) * 128)
                first = pl.multiple_of(whose[side] * width + pair * 128, 128)
                size = sizes[side]
                result = mm(keys[pl.ds(starts[side], size), at], query[pl.ds(first, 128), :])
                scores[side, :size, pair * 256 : (pair + 1) * 256] = result

            def soften(side, pair):
                at = slice(pair * 256, (pair + 1) * 256)
                size = sizes[side]
                live = positions[side] < lengths[side]
                score = jnp.where(live, scores[side, :size, at], -1e30)
                power = jnp.exp(score - jnp.max(score, axis=0, keepdims=True))
                weights[side, :size, at] = power.astype(BF)
                scale = 1.0 / jnp.sum(power, axis=0, keepdims=True)
                scales[side, 0:1, at] = jnp.where(lengths[side] > 0, scale, 0.0)

            def gather(side, pair):
                at = slice(pair * 256, (pair + 1) * 256)
                size = sizes[side]
                v = values[pl.ds(starts[side], size), pair * 128 : (pair + 1) * 128]
                w = weights[side, :size, at]
                result = lax.dot_general(v, w, DOWN, preferred_element_type=F32)
                scale = scales[side, 0:1, at]
                to = pl.multiple_of(whose[side] * width + pair * 128, 128)
                context[pl.ds(to, 64), :] += result[:64, :128] * scale[:, :128]
                context[pl.ds(to + 64, 64), :] += result[64:, 128:] * scale[:, 128:]

            for pair in pairs:
                score(0, pair)
            for pair in pairs:
                score(1, pair)
                soften(0, pair)
            for pair in pairs:
                soften(1, pair)
                gather(0, pair)
            for pair in pairs:
                gather(1, pair)

        longer = [length > 64 for length in lengths]

        @pl.when(longer[1])
        def _():
            with_keys(128, 128)

        @pl.when(jnp.logical_and(longer[0], jnp.logical_not(longer[1])))
        def _():
            with_keys(128, 64)

        @pl.when(jnp.logical_not(jnp.logical_or(longer[0], longer[1])))
        def _():
            with_keys(64, 64)

        return carry

    lax.fori_loop(0, (meta[0, 3] + 1) // 2, two_sides, 0)
    copies[4].wait()
    part = context[width:, :].astype(BF)
    update = lax.dot_general(part, weight_o[...], DOWN, preferred_element_type=F32)
    sibling[...] = jnp.where(iota(update.shape, 0) < meta[0, 5], update, 0.0).astype(BF)
    leave = [copy(9, sibling, sibling_at)]
    leave[0].start()
    part = context[:width, :].astype(BF)
    for half in range(2):
        at = pl.ds(half * (width // 2), width // 2)
        update = lax.dot_general(part, weight_o[:, at], DOWN, preferred_element_type=F32)
        out[:, at] = jnp.where(iota(update.shape, 0) < meta[0, 4], update, 0.0)
        leave.append(copy(10 + half, out.at[:, at], out_at.at[:, at]))
        leave[-1].start()
    for one in leave:
        one.wait()


def attend(meta, got, query, weight_k, weight_v, weight_o):
    width = weight_k.shape[0]
    each = 1
    for n in got.shape[1:-1]:
        each *= n
    tall = 2 * each * BLOCK
    return pl.pallas_call(
        attend_kernel,
        out_shape=(
            jax.ShapeDtypeStruct((128, width), F32),
            jax.ShapeDtypeStruct((128, width), BF),
        ),
        in_specs=[HBM] * 6,
        out_specs=(HBM, HBM),
        scratch_shapes=[
            pltpu.SMEM(meta.shape, jnp.int32),
            pltpu.VMEM(got.shape, BF),
            pltpu.VMEM(query.shape, BF),
            pltpu.VMEM((width, width), BF),
            pltpu.VMEM((width, width), BF),
            pltpu.VMEM((width, width), BF),
            pltpu.VMEM((tall, width), BF),
            pltpu.VMEM((tall + (PARTS - 1) * BLOCK, width), BF),
            pltpu.VMEM((tall + (PARTS - 1) * BLOCK, width), BF),
            pltpu.VMEM((2 * width, 128), F32),
            pltpu.VMEM((2, 128, 2 * width), F32),
            pltpu.VMEM((2, 128, 2 * width), BF),
            pltpu.VMEM((2, 8, 2 * width), F32),
            pltpu.VMEM((128, width), F32),
            pltpu.VMEM((128, width), BF),
            pltpu.SemaphoreType.DMA((12,)),
        ],
        compiler_params=pltpu.CompilerParams(vmem_limit_bytes=36 * MIB),
        cost_estimate=pl.CostEstimate(flops=10**10, bytes_accessed=10**7, transcendentals=10**6),
    )(meta, got, query, weight_k, weight_v, weight_o)


def later_round(number, sides, me, count, meta):
    dest, source, length, amount, base, _, place, _ = sides
    origin = FIRST - PARTS + 1
    turn = jnp.where(base + amount <= FIRST, 0, 1 + (base - origin) // STEP)
    active = turn == number
    base = base - origin - (number - 1) * STEP
    spots = jnp.arange(LATER, dtype=jnp.int32)
    target = (dest[None, :] == jnp.arange(count, dtype=jnp.int32)[:, None]) & active[None, :]
    there = (base[:, None] <= spots) & (spots < (base + amount)[:, None])
    entries = [jnp.where(there, source[:, None] + 1, 0), jnp.where(there, spots - base[:, None], 0)]
    high, low = (mm(target.astype(BF), entry.astype(BF)).astype(jnp.int32) for entry in entries)
    unit = (4 * (high - 1) + low).reshape(-1, 2)
    columns = jnp.arange(2 * count, dtype=jnp.int32)
    selector = jnp.where((unit // 2)[:, :, None] == columns, (1 - 2 * (unit % 2))[:, :, None], 0)
    selector = selector.reshape(unit.shape[0], -1).astype(BF)
    held = active & (dest == me)
    order = jnp.sum(held[:, None] & (base[:, None] < base[None, :]), axis=0)
    chosen = held[None, :] & (order[None, :] == spots[:, None])

    def listed(values):
        return jnp.sum(jnp.where(chosen, values[None, :], 0), axis=1)

    held_count = jnp.broadcast_to(jnp.sum(held.astype(jnp.int32)), (LATER,))
    columns = [listed(base), listed(length), listed((place + me) % 2), held_count]
    meta = meta[:LATER].at[:, :4].set(jnp.stack(columns, axis=1))
    return selector, meta.at[:, 7].set(jnp.max(jnp.where(held, base + amount, 0)))


def local(embeddings, weight_q, weight_k, weight_v, weight_o, pairs, lengths, holder):
    count = lax.axis_size("group") * lax.axis_size("dev")
    me = lax.axis_index("group") * lax.axis_size("dev") + lax.axis_index("dev")
    own = embeddings[0]
    mine = exchange(front(own))
    selector, meta, sides = plan(me, pairs, lengths, holder)
    rounds = meta[0, 6]
    query = queries(own, swap(own), weight_q)

    def one_round(selector, meta, mine, outer):
        got = exchange(pick(selector, mine, outer))
        return attend(meta, got, query, weight_k, weight_v, weight_o)

    def another(carry):
        number, total = carry
        kept, given = one_round(*later_round(number, sides, me, count, meta), exchange(front(own)), (LATER // 2,))
        return number + 1, total + kept + swap(given).astype(F32)

    kept, given = one_round(selector, meta, mine, (FIRST // 8, 4))
    received = swap(given)
    _, kept = lax.while_loop(lambda c: c[0] <= rounds, another, (jnp.int32(1), kept))
    return (own.astype(F32) + (kept + received.astype(F32))).astype(BF)[None]


def solution(mesh):
    in_specs = (P(AXES, None, None), P(), P(), P(), P(), P(), P(), P())
    out_specs = P(AXES, None, None)
    return jax.shard_map(local, mesh=mesh, in_specs=in_specs, out_specs=out_specs, check_vma=False)
```
